32 devices in a mesh: dp: 8 (over y, x, core), fsdp: 4 (over z).
Axes of the slice: x: 2, y: 2, z: 4, core: 2. Of those that a mesh axis runs over, the one named last changes fastest.
Arguments:
- single: bfloat16 [96, 384, 768], P(('dp', 'fsdp')), may hold values from -6 to 6
- condition: bfloat16 [96, 384, 384], P(('dp', 'fsdp')), may hold values from -6 to 6
- pair_tensor: bfloat16 [2, 384, 384, 128], P(None, 'dp', 'fsdp'), may hold values from -6 to 6
- counts: int32 [2], replicated, may hold values from 96 to 384, as said below
- complex_of: int32 [96], P(('dp', 'fsdp')), may hold values from 0 to 1
- cotangent: bfloat16 [96, 384, 768], P(('dp', 'fsdp')), may hold values from -6 to 6
- condition_gain: bfloat16 [384], P('fsdp'), may hold values from 0.099609375 to 1.8984375
- scale_weight: bfloat16 [384, 768], P('fsdp'), may hold values from -0.3125 to 0.3125
- scale_bias: bfloat16 [768], P('fsdp'), may hold values from -4 to 4
- shift_weight: bfloat16 [384, 768], P('fsdp'), may hold values from -0.3125 to 0.3125
- query_weight: bfloat16 [768, 768], P('fsdp'), may hold values from -0.3125 to 0.3125
- query_bias: bfloat16 [768], P('fsdp'), may hold values from -3 to 3
- key_weight: bfloat16 [768, 768], P('fsdp'), may hold values from -0.3125 to 0.3125
- value_weight: bfloat16 [768, 768], P('fsdp'), may hold values from -0.21875 to 0.21875
- gate_weight: bfloat16 [768, 768], P('fsdp'), may hold values from -0.21875 to 0.21875
- output_weight: bfloat16 [768, 768], P('fsdp'), may hold values from -2.5 to 2.5
- pair_gain: bfloat16 [128], P('fsdp'), may hold values from 0.099609375 to 1.8984375
- pair_weight: bfloat16 [128, 16], P('fsdp'), may hold values from -0.5 to 0.5
- branch_gate_weight: bfloat16 [384, 768], P('fsdp'), may hold values from -0.3125 to 0.3125
- branch_gate_bias: bfloat16 [768], P('fsdp'), may hold values from -4 to 4
- transition_gain: bfloat16 [384], P('fsdp'), may hold values from 0.099609375 to 1.8984375
- transition_scale_weight: bfloat16 [384, 768], P('fsdp'), may hold values from -0.3125 to 0.3125
- transition_scale_bias: bfloat16 [768], P('fsdp'), may hold values from -4 to 4
- transition_shift_weight: bfloat16 [384, 768], P('fsdp'), may hold values from -0.3125 to 0.3125
- hidden_gate: bfloat16 [768, 1536], P('fsdp'), may hold values from -0.21875 to 0.21875
- hidden_value: bfloat16 [768, 1536], P('fsdp'), may hold values from -0.21875 to 0.21875
- hidden_output: bfloat16 [1536, 768], P('fsdp'), may hold values from -0.3125 to 0.3125
- final_gate_weight: bfloat16 [384, 768], P('fsdp'), may hold values from -0.3125 to 0.3125
- final_gate_bias: bfloat16 [768], P('fsdp'), may hold values from -4 to 4
Outputs:
- output: bfloat16 [96, 384, 768], P(('dp', 'fsdp'))
- single_grad: float32 [96, 384, 768], P(('dp', 'fsdp'))
- condition_grad: float32 [96, 384, 384], P(('dp', 'fsdp'))
- pair_grad: float32 [2, 384, 384, 128], P(None, 'dp', 'fsdp')
- condition_gain_grad: float32 [384], P('fsdp')
- scale_weight_grad: float32 [384, 768], P('fsdp')
- scale_bias_grad: float32 [768], P('fsdp')
- shift_weight_grad: float32 [384, 768], P('fsdp')
- query_weight_grad: float32 [768, 768], P('fsdp')
- query_bias_grad: float32 [768], P('fsdp')
- key_weight_grad: float32 [768, 768], P('fsdp')
- value_weight_grad: float32 [768, 768], P('fsdp')
- gate_weight_grad: float32 [768, 768], P('fsdp')
- output_weight_grad: float32 [768, 768], P('fsdp')
- pair_gain_grad: float32 [128], P('fsdp')
- pair_weight_grad: float32 [128, 16], P('fsdp')
- branch_gate_weight_grad: float32 [384, 768], P('fsdp')
- branch_gate_bias_grad: float32 [768], P('fsdp')
- transition_gain_grad: float32 [384], P('fsdp')
- transition_scale_weight_grad: float32 [384, 768], P('fsdp')
- transition_scale_bias_grad: float32 [768], P('fsdp')
- transition_shift_weight_grad: float32 [384, 768], P('fsdp')
- hidden_gate_grad: float32 [768, 1536], P('fsdp')
- hidden_value_grad: float32 [768, 1536], P('fsdp')
- hidden_output_grad: float32 [1536, 768], P('fsdp')
- final_gate_weight_grad: float32 [384, 768], P('fsdp')
- final_gate_bias_grad: float32 [768], P('fsdp')
The draws below stay inside these ranges and needn't reach their ends.
Inputs may be any that keep to these rules, and one draw needn't show every extreme that they name: `counts`: token slots at and beyond a complex's count are padding; one complex in each draw has exactly 384 tokens.
All inputs are finite; a program needn't handle non-finite values.
Results may differ from the reference program's by a relative error of at most 0.025.
Values may be sent and summed in bfloat16 or wider, within the bound.
A program may use at most 320 MiB of HBM per device.

```python
import jax
import jax.numpy as jnp
from jax import lax

D = 768
DC = 384
DP = 128
H = 16
FF = 1536
NCOMP = 2
LMAX = 384
COPIES = 96


def draw_counts(key, part):
    key = jax.random.fold_in(key, 7)
    base_key, pick_key = jax.random.split(key)
    drawn = jax.random.randint(base_key, (NCOMP,), LMAX // 4, LMAX + 1)
    longest = jax.random.randint(pick_key, (), 0, NCOMP)
    return jnp.where(jnp.arange(NCOMP) == longest, LMAX, drawn).astype(jnp.int32)


def touch_ends(values, stream_key, low, high):
    longest = values.shape.index(max(values.shape))
    spots = []
    for shift in (0, 1):
        where = [jax.random.randint(jax.random.fold_in(stream_key, axis), (), 0, length) for axis, length in enumerate(values.shape)]
        where[longest] = (where[longest] + shift) % values.shape[longest]
        spots.append(tuple(where))
    return values.at[spots[0]].set(low).at[spots[1]].set(high)


def block_scale(own_key, shape, cuts, low, largest):
    def one(axis_at, shards_of):
        steps = jax.random.uniform(jax.random.fold_in(jax.random.fold_in(own_key, 6), axis_at), (shards_of,), jnp.float32, low / len(cuts), largest / len(cuts))
        return jnp.repeat(jnp.exp(steps), shape[axis_at] // shards_of).reshape((-1,) + (1,) * (len(shape) - axis_at - 1))

    loudness = one(*cuts[0])
    for cut in cuts[1:]:
        loudness = loudness * one(*cut)
    return loudness


def gaussian(rng, dims, spread, most, cuts=(), kind=jnp.bfloat16):
    entries = jax.random.normal(rng, dims, jnp.float32) * spread
    if len(cuts) > 0:
        entries = block_scale(rng, dims, cuts, -0.22, 0.18) * entries
    return jnp.clip(entries, min=-most, max=most).astype(kind)


def setup_inputs(seed: int = 0) -> dict:
    splits = jax.random.split(jax.random.key(seed), 30)
    return {
        "single": gaussian(splits[0], (COPIES, LMAX, D), 1.0, 6.0, ((0, 32),)),
        "condition": gaussian(splits[1], (COPIES, LMAX, DC), 1.0, 6.0, ((0, 32),)),
        "pair_tensor": gaussian(splits[2], (NCOMP, LMAX, LMAX, DP), 1.0, 6.0, ((1, 8), (2, 4))),
        "counts": draw_counts(jax.random.fold_in(splits[29], 71), 0),
        "complex_of": touch_ends(jax.random.randint(splits[4], (COPIES,), 0, NCOMP), jax.random.fold_in(splits[4], 1), 0, NCOMP - 1).astype(jnp.int32),
        "cotangent": gaussian(splits[5], (COPIES, LMAX, D), 1.0, 6.0, ((0, 32),)),
        "condition_gain": jnp.clip(1.0 + 0.18 * jax.random.normal(splits[6], (DC,), jnp.float32), 0.099609375, 1.8984375).astype(jnp.bfloat16),
        "scale_weight": gaussian(splits[7], (DC, D), DC ** -0.5, 0.3125, ((0, 4),)),
        "scale_bias": gaussian(splits[8], (D,), 1.0, 4.0, ((0, 4),)),
        "shift_weight": gaussian(splits[9], (DC, D), DC ** -0.5, 0.3125, ((0, 4),)),
        "query_weight": gaussian(splits[10], (D, D), (D // 2) ** -0.5, 0.3125, ((0, 4),)),
        "query_bias": gaussian(splits[11], (D,), 0.5, 3.0, ((0, 4),)),
        "key_weight": gaussian(splits[12], (D, D), (D // 2) ** -0.5, 0.3125, ((0, 4),)),
        "value_weight": gaussian(splits[13], (D, D), D ** -0.5, 0.21875, ((0, 4),)),
        "gate_weight": gaussian(splits[14], (D, D), D ** -0.5, 0.21875, ((0, 4),)),
        "output_weight": gaussian(splits[15], (D, D), (max(D // 128, 1)) ** -0.5, 2.5, ((0, 4),)),
        "pair_gain": jnp.clip(1.0 + 0.18 * jax.random.normal(splits[16], (DP,), jnp.float32), 0.099609375, 1.8984375).astype(jnp.bfloat16),
        "pair_weight": gaussian(splits[17], (DP, H), DP ** -0.5, 0.5, ((0, 4),)),
        "branch_gate_weight": gaussian(splits[18], (DC, D), DC ** -0.5, 0.3125, ((0, 4),)),
        "branch_gate_bias": gaussian(splits[19], (D,), 1.0, 4.0, ((0, 4),)),
        "transition_gain": jnp.clip(1.0 + 0.18 * jax.random.normal(splits[20], (DC,), jnp.float32), 0.099609375, 1.8984375).astype(jnp.bfloat16),
        "transition_scale_weight": gaussian(splits[21], (DC, D), DC ** -0.5, 0.3125, ((0, 4),)),
        "transition_scale_bias": gaussian(splits[22], (D,), 1.0, 4.0, ((0, 4),)),
        "transition_shift_weight": gaussian(splits[23], (DC, D), DC ** -0.5, 0.3125, ((0, 4),)),
        "hidden_gate": gaussian(splits[24], (D, FF), D ** -0.5, 0.21875, ((0, 4),)),
        "hidden_value": gaussian(splits[25], (D, FF), D ** -0.5, 0.21875, ((0, 4),)),
        "hidden_output": gaussian(splits[26], (FF, D), (FF // 4) ** -0.5, 0.3125, ((0, 4),)),
        "final_gate_weight": gaussian(splits[27], (DC, D), DC ** -0.5, 0.3125, ((0, 4),)),
        "final_gate_bias": gaussian(splits[28], (D,), 1.0, 4.0, ((0, 4),)),
    }


@jax.custom_vjp
def low(v):
    return lax.optimization_barrier(v.astype(jnp.bfloat16)).astype(jnp.float32)

@jax.custom_vjp
def low_back(v):
    return v

def low_keep(v):
    return (low(v), None)

def low_pass(kept, grad):
    return (grad,)

def back_keep(v):
    return (v, None)

def back_low(kept, grad):
    return (low(grad),)
low.defvjp(low_keep, low_pass)
low_back.defvjp(back_keep, back_low)
EPSILON = 1e-05
HIGHEST = lax.Precision.HIGHEST
WEIGHT_NAMES = ('condition_gain', 'scale_weight', 'scale_bias', 'shift_weight', 'query_weight', 'query_bias', 'key_weight', 'value_weight', 'gate_weight', 'output_weight', 'pair_gain', 'pair_weight', 'branch_gate_weight', 'branch_gate_bias', 'transition_gain', 'transition_scale_weight', 'transition_scale_bias', 'transition_shift_weight', 'hidden_gate', 'hidden_value', 'hidden_output', 'final_gate_weight', 'final_gate_bias')

def matmul(left, right):
    return jnp.dot(left, right, precision=HIGHEST)

def normed(values):
    centred = values - lax.optimization_barrier(jnp.mean(values, axis=-1, keepdims=True))
    return centred * lax.rsqrt(lax.optimization_barrier(jnp.mean(centred * centred, axis=-1, keepdims=True)) + EPSILON)

def ada_norm(hidden, condition_in, gain, scale_matrix, scale_offset, shift_matrix):
    condition_low = low(normed(condition_in) * gain)
    scale_pre = low_back(matmul(condition_low, scale_matrix) + scale_offset)
    shift_pre = low_back(matmul(condition_low, shift_matrix))
    return low(jax.nn.sigmoid(scale_pre) * normed(hidden) + shift_pre)

def block(weights, single_in, condition_in, keep_mask, pair_bias):
    copy_count, row_count, model_width = single_in.shape
    head_count = weights['pair_weight'].shape[1]
    head_size = model_width // head_count
    first_in = ada_norm(single_in, condition_in, weights['condition_gain'], weights['scale_weight'], weights['scale_bias'], weights['shift_weight'])
    queries = low(low_back(matmul(first_in, weights['query_weight']) + weights['query_bias']))
    key_rows = low(low_back(matmul(first_in, weights['key_weight'])))
    value_rows = low(low_back(matmul(first_in, weights['value_weight'])))
    gate_pre = low_back(matmul(first_in, weights['gate_weight']))
    shaped = (copy_count, row_count, head_count, head_size)
    scores = jnp.einsum('clhe,cmhe->chlm', queries.reshape(shaped), key_rows.reshape(shaped), precision=HIGHEST)
    scores = low_back(scores * head_size ** (-0.5) + pair_bias)
    scores = jnp.where(keep_mask[:, None, None, :] > 0, scores, -1000000000.0)
    softmaxed = low(jax.nn.softmax(scores, axis=-1))
    attended = jnp.einsum('chlm,cmhe->clhe', softmaxed, value_rows.reshape(shaped), precision=HIGHEST)
    attended = low_back(attended.reshape(copy_count, row_count, model_width))
    gated_low = low(jax.nn.sigmoid(gate_pre) * attended)
    branch_one = low_back(matmul(gated_low, weights['output_weight']))
    zero_one = jax.nn.sigmoid(low_back(matmul(condition_in, weights['branch_gate_weight']) + weights['branch_gate_bias']))
    middle = single_in + keep_mask[..., None] * zero_one * branch_one
    second_in = ada_norm(middle, condition_in, weights['transition_gain'], weights['transition_scale_weight'], weights['transition_scale_bias'], weights['transition_shift_weight'])
    hidden_pre = low_back(matmul(second_in, weights['hidden_gate']))
    value_pre = low_back(matmul(second_in, weights['hidden_value']))
    activated = low(jax.nn.silu(hidden_pre) * value_pre)
    branch_two = low_back(matmul(activated, weights['hidden_output']))
    zero_two = jax.nn.sigmoid(low_back(matmul(condition_in, weights['final_gate_weight']) + weights['final_gate_bias']))
    return middle + keep_mask[..., None] * zero_two * branch_two

def reference(single, condition, pair_tensor, counts, complex_of, cotangent, condition_gain, scale_weight, scale_bias, shift_weight, query_weight, query_bias, key_weight, value_weight, gate_weight, output_weight, pair_gain, pair_weight, branch_gate_weight, branch_gate_bias, transition_gain, transition_scale_weight, transition_scale_bias, transition_shift_weight, hidden_gate, hidden_value, hidden_output, final_gate_weight, final_gate_bias):
    initials = [single, condition, pair_tensor, condition_gain, scale_weight, scale_bias, shift_weight, query_weight, query_bias, key_weight, value_weight, gate_weight, output_weight, pair_gain, pair_weight, branch_gate_weight, branch_gate_bias, transition_gain, transition_scale_weight, transition_scale_bias, transition_shift_weight, hidden_gate, hidden_value, hidden_output, final_gate_weight, final_gate_bias]
    floats = [values.astype(jnp.float32) for values in initials]
    positions = jnp.arange(LMAX, dtype=jnp.int32)
    copy_lengths = counts[complex_of].astype(jnp.int32)
    keep_mask = (positions[None, :] < copy_lengths[:, None]).astype(jnp.float32)
    group_count = single.shape[0] // 8

    def forward(*inputs):
        single_in, condition_in, pair_in = (inputs[0], inputs[1], inputs[2])
        weights = dict(zip(WEIGHT_NAMES, inputs[3:]))
        pair_low = low(normed(pair_in) * weights['pair_gain'])
        pair_bias = low(low_back(matmul(pair_low, weights['pair_weight'])))
        pair_bias = jnp.transpose(pair_bias, (0, 3, 1, 2))

        def one_group(pieces):
            single_part, condition_part, keep_part, complex_part = pieces
            return block(weights, single_part, condition_part, keep_part, pair_bias[complex_part])
        stacked = lax.map(jax.checkpoint(one_group), (single_in.reshape(group_count, 8, LMAX, D), condition_in.reshape(group_count, 8, LMAX, DC), keep_mask.reshape(group_count, 8, LMAX), complex_of.reshape(group_count, 8)))
        return stacked.reshape(group_count * 8, LMAX, D)
    output, pullback = jax.vjp(forward, *floats)
    gradients = pullback(cotangent.astype(jnp.float32))
    return (output.astype(jnp.bfloat16), gradients[0], gradients[1], gradients[2], gradients[3], gradients[4], gradients[5], gradients[6], gradients[7], gradients[8], gradients[9], gradients[10], gradients[11], gradients[12], gradients[13], gradients[14], gradients[15], gradients[16], gradients[17], gradients[18], gradients[19], gradients[20], gradients[21], gradients[22], gradients[23], gradients[24], gradients[25])
```

```python
import functools

import jax
import jax.numpy as jnp
from jax import lax
from jax.experimental import pallas as pl
from jax.experimental.pallas import tpu as pltpu
from jax.sharding import PartitionSpec as P

BF = jnp.bfloat16
F32 = jnp.float32
EPSILON = 1e-05
DP = "dp"
FS = "fsdp"
MIB = 1024 * 1024
NEGATIVE = -1000000000.0


def norm(v):
    c = v - jnp.mean(v, axis=-1, keepdims=True)
    r = lax.rsqrt(jnp.mean(c * c, axis=-1, keepdims=True) + EPSILON)
    return c * r, r


def norm_back(n, r, u):
    return r * (u - jnp.mean(u, axis=-1, keepdims=True) - n * jnp.mean(u * n, axis=-1, keepdims=True))


def sig(v):
    return 0.5 * jnp.tanh(0.5 * v) + 0.5


def dot(a, b):
    return jnp.dot(a, b, preferred_element_type=F32)


def dot_nt(a, b):
    return lax.dot_general(a, b, (((1,), (1,)), ((), ())), preferred_element_type=F32)


def dot_tn(a, b):
    return lax.dot_general(a, b, (((0,), (0,)), ((), ())), preferred_element_type=F32)


def flat(ref):
    v = ref[...]
    return v.reshape(v.shape[0] * v.shape[1], v.shape[2])


def colsum(v):
    return jnp.sum(v.astype(F32), axis=0, keepdims=True)


def first_kernel(x, c, wq, wk, wv, wg, ws, wh, sm, fi, q, k, v, gp, sp, cl):
    cn, _ = norm(c[...].astype(F32))
    low = (cn * sm[5:6, : cn.shape[1]]).astype(BF)
    cl[...] = low
    pre = dot(low, flat(ws)) + sm[0:1, :]
    shift = dot(low, flat(wh))
    sp[...] = pre.astype(BF)
    an, _ = norm(x[...].astype(F32))
    first = (sig(pre) * an + shift).astype(BF)
    fi[...] = first
    q[...] = (dot(first, flat(wq)) + sm[1:2, :]).astype(BF)
    k[...] = dot(first, flat(wk)).astype(BF)
    v[...] = dot(first, flat(wv)).astype(BF)
    gp[...] = dot(first, flat(wg)).astype(BF)


def whole(shape):
    return pl.BlockSpec(shape, lambda *i: (0,) * len(shape), pipeline_mode=pl.Buffered(1))


def part(z, rows, width, at):
    return pl.BlockSpec((z, rows, width), lambda *i: (0, at, 0), pipeline_mode=pl.Buffered(1))


def rows_of(tb, width):
    return pl.BlockSpec((tb, width), lambda i, *_: (i, 0))


def params(limit, **kw):
    return pltpu.CompilerParams(vmem_limit_bytes=limit * MIB, **kw)


def cost(flops, nbytes, trans=0):
    return pl.CostEstimate(flops=int(flops), bytes_accessed=int(nbytes), transcendentals=int(trans))


def run_first(x, c, g1, sm, tb):
    t, d = x.shape
    dc = c.shape[1]
    z = g1.shape[0]
    dz, cz = d // z, dc // z
    sds = jax.ShapeDtypeStruct
    return pl.pallas_call(
        first_kernel,
        grid=(t // tb,),
        in_specs=[rows_of(tb, d), rows_of(tb, dc)]
        + [part(z, dz, d, i) for i in range(4)]
        + [part(z, cz, d, 4 * dz // cz), part(z, cz, d, 4 * dz // cz + 1), whole(sm.shape)],
        out_specs=[rows_of(tb, d)] * 6 + [rows_of(tb, dc)],
        out_shape=[sds((t, d), BF)] * 6 + [sds((t, dc), BF)],
        compiler_params=params(60),
        cost_estimate=cost(2 * t * d * (4 * d + 2 * dc), 20 * MIB),
        name="first",
    )(x, c, g1, g1, g1, g1, g1, g1, sm)


def windows(per, hs):
    out = []
    for j in range(per):
        lo = j * hs
        w = min(lo // 128 * 128, max(per * hs - 256, 0))
        out.append((w, lo - w))
    return out


def lane_mask(o, hs, width):
    lane = lax.broadcasted_iota(jnp.int32, (1, width), 1)
    return jnp.where((lane >= o) & (lane < o + hs), 1.0, 0.0).astype(BF)


def put(acc, w, width, val):
    for b in range(width // 128):
        key = w // 128 + b
        piece = val[:, 128 * b : 128 * b + 128]
        acc[key] = piece if key not in acc else acc[key] + piece


def attend_kernel(per, hs, comp, cnt, q, k, v, b, gp, p_out, att, gated):
    n = comp[pl.program_id(0)]
    width = min(256, per * hs)
    limit = cnt[n]
    mrow = jnp.where(
        lax.broadcasted_iota(jnp.int32, (1, k.shape[0]), 1) < limit, 0.0, NEGATIVE
    ).astype(F32)
    scale = hs ** (-0.5)
    acc = {}
    for j, (w, o) in enumerate(windows(per, hs)):
        m = lane_mask(o, hs, width)
        s = dot_nt(q[:, w : w + width] * m, k[:, w : w + width]) * scale
        s = s + (b[0, j].astype(F32) + mrow)
        e = jnp.exp(s - jnp.max(s, axis=-1, keepdims=True))
        pb = (e * (1.0 / jnp.sum(e, axis=-1, keepdims=True))).astype(BF)
        p_out[0, j] = pb
        put(acc, w, width, dot(pb, v[:, w : w + width] * m))
    for key, val in acc.items():
        cols = slice(128 * key, 128 * key + 128)
        att[:, cols] = val.astype(BF)
        gated[:, cols] = (sig(gp[:, cols].astype(F32)) * val).astype(BF)


def run_attend(comp, cnt, q, k, v, gp, bias, groups):
    copies = comp.shape[0]
    t, d = q.shape
    rows = t // copies
    heads = bias.shape[1]
    per, dg = heads // groups, d // groups
    blk = pl.BlockSpec((rows, dg), lambda c, g, *_: (c, g))
    sds = jax.ShapeDtypeStruct
    return pl.pallas_call(
        functools.partial(attend_kernel, per, d // heads),
        grid_spec=pltpu.PrefetchScalarGridSpec(
            num_scalar_prefetch=2,
            grid=(copies, groups),
            in_specs=[
                blk,
                blk,
                blk,
                pl.BlockSpec((1, per, rows, rows), lambda c, g, comp, cnt: (comp[c], g, 0, 0)),
                blk,
            ],
            out_specs=[
                pl.BlockSpec((1, per, rows, rows), lambda c, g, *_: (c, g, 0, 0)),
                blk,
                blk,
            ],
        ),
        out_shape=[sds((copies, heads, rows, rows), BF), sds((t, d), BF), sds((t, d), BF)],
        compiler_params=params(60),
        cost_estimate=cost(2 * 2 * t * rows * heads * 256, 40 * MIB, t * rows * heads),
        name="attend",
    )(comp, cnt, q, k, v, bias, gp)


def attend_back_kernel(per, hs, comp, p, q, k, v, da, at, dq, dk, dv, db, acc):
    c = pl.program_id(1)
    last = pl.num_programs(1) - 1
    n = comp[c]
    width = min(256, per * hs)
    scale = hs ** (-0.5)

    @pl.when(c == 0)
    def _():
        acc[...] = jnp.zeros_like(acc)

    aq, ak, av = {}, {}, {}
    prod = da[...].astype(F32) * at[...].astype(F32)
    lane = lax.broadcasted_iota(jnp.int32, (1, per * hs), 1)
    for j, (w, o) in enumerate(windows(per, hs)):
        m = lane_mask(o, hs, width)
        lo = w + o
        inside = (lane >= lo) & (lane < lo + hs)
        delta = jnp.sum(jnp.where(inside, prod, 0.0), axis=-1, keepdims=True)
        pj = p[0, j]
        win = slice(w, w + width)
        dam = da[:, win] * m
        dp = dot_nt(dam, v[:, win])
        ds = pj.astype(F32) * (dp - delta)
        acc[n, j] += ds
        dsb = ds.astype(BF)
        put(av, w, width, dot_tn(pj, dam))
        put(aq, w, width, dot(dsb, k[:, win] * m))
        put(ak, w, width, dot_tn(dsb, q[:, win] * m))
    for key in aq:
        cols = slice(128 * key, 128 * key + 128)
        dq[:, cols] = (aq[key] * scale).astype(BF)
        dk[:, cols] = (ak[key] * scale).astype(BF)
        dv[:, cols] = av[key].astype(BF)

    @pl.when(c == last)
    def _():
        db[...] = acc[...].astype(BF)


def run_attend_back(comp, p, q, k, v, da, att, ncomp, groups):
    copies, heads, rows, _ = p.shape
    t, d = q.shape
    per, dg = heads // groups, d // groups
    blk = pl.BlockSpec((rows, dg), lambda g, c, *_: (c, g))
    sds = jax.ShapeDtypeStruct
    return pl.pallas_call(
        functools.partial(attend_back_kernel, per, d // heads),
        grid_spec=pltpu.PrefetchScalarGridSpec(
            num_scalar_prefetch=1,
            grid=(groups, copies),
            in_specs=[pl.BlockSpec((1, per, rows, rows), lambda g, c, *_: (c, g, 0, 0))]
            + [blk] * 5,
            out_specs=[blk] * 3
            + [
                pl.BlockSpec(
                    (ncomp, per, rows, rows),
                    lambda g, c, *_: (0, g, 0, 0),
                    pipeline_mode=pl.Buffered(1),
                )
            ],
            scratch_shapes=[pltpu.VMEM((ncomp, per, rows, rows), F32)],
        ),
        out_shape=[sds((t, d), BF)] * 3 + [sds((ncomp, heads, rows, rows), BF)],
        compiler_params=params(60),
        cost_estimate=cost(4 * 2 * t * rows * heads * 256, 40 * MIB),
        name="attend_back",
    )(comp, p, q, k, v, da, att)


def middle_kernel(per_copy, comp, cnt, x, c, ct, gat, att, gp, wo, hl, hr, vl, vr, ho, bg, ts, th, fg, sm,
                  out, gm_o, dc_o, si_o, act_o, cl_o, g2_o, gz2_o, gh_o, gv_o, gsc_o, gsh_o, g1_o, gz1_o, da_o, dg_o, vec):
    i = pl.program_id(0)
    tb, d = x.shape
    dc = c.shape[1]
    copy = i // per_copy
    limit = cnt[comp[copy]] - (i % per_copy) * tb
    keep = jnp.where(lax.broadcasted_iota(jnp.int32, (tb, 1), 0) < limit, 1.0, 0.0).astype(F32)

    low = c[...]
    y1 = dot(gat[...], flat(wo))
    z1 = sig(dot(low, flat(bg)) + sm[2:3, :])
    kz1 = keep * z1
    mid = x[...].astype(F32) + kz1 * y1
    cn, cr = norm(low.astype(F32))
    gain = sm[6:7, :dc]
    cl = (cn * gain).astype(BF)
    cl_o[...] = cl
    s2 = sig(dot(cl, flat(ts)) + sm[3:4, :])
    mn, mr = norm(mid)
    si = (s2 * mn + dot(cl, flat(th))).astype(BF)
    si_o[...] = si
    zh = ho.shape[0] // 2
    kept = []
    y2 = None
    for half, (hg, hv) in enumerate(((hl, vl), (hr, vr))):
        u = dot(si, flat(hg))
        w = dot(si, flat(hv))
        su = sig(u)
        silu = u * su
        act = (silu * w).astype(BF)
        act_o[:, half * d : half * d + d] = act
        kept.append((w * su * (1.0 + u - silu), silu))
        hov = ho[half * zh : half * zh + zh]
        term = dot(act, hov.reshape(d, d))
        y2 = term if y2 is None else y2 + term
    z2 = sig(dot(low, flat(fg)) + sm[4:5, :])
    g = ct[...].astype(F32)
    kz2 = keep * z2
    out[...] = (mid + kz2 * y2).astype(BF)
    gk = g * kz2
    g2 = gk.astype(BF)
    gz2 = (gk * y2 * (1.0 - z2)).astype(BF)
    g2_o[...] = g2
    gz2_o[...] = gz2
    e = None
    for half, (hg, hv) in enumerate(((hl, vl), (hr, vr))):
        hov = ho[half * zh : half * zh + zh]
        ga = dot_nt(g2, hov.reshape(d, d))
        du, silu = kept[half]
        gh = (ga * du).astype(BF)
        gv = (ga * silu).astype(BF)
        gh_o[:, half * d : half * d + d] = gh
        gv_o[:, half * d : half * d + d] = gv
        term = dot_nt(gh, flat(hg)) + dot_nt(gv, flat(hv))
        e = term if e is None else e + term
    t = e * s2
    gsc = (t * mn * (1.0 - s2)).astype(BF)
    gsh = e.astype(BF)
    gsc_o[...] = gsc
    gsh_o[...] = gsh
    gc = dot_nt(gsc, flat(ts)) + dot_nt(gsh, flat(th))
    gm = g + norm_back(mn, mr, t)
    gm_o[...] = gm
    kz = gm * kz1
    g1 = kz.astype(BF)
    gz1 = (kz * y1 * (1.0 - z1)).astype(BF)
    g1_o[...] = g1
    gz1_o[...] = gz1
    dc_o[...] = norm_back(cn, cr, gc * gain) + dot_nt(gz2, flat(fg)) + dot_nt(gz1, flat(bg))
    gg = dot_nt(g1, flat(wo))
    sp = sig(gp[...].astype(F32))
    da = gg * sp
    da_o[...] = da.astype(BF)
    dg_o[...] = (da * att[...].astype(F32) * (1.0 - sp)).astype(BF)

    @pl.when(i == 0)
    def _():
        vec[...] = jnp.zeros_like(vec)

    vec[2:3, :] += colsum(gz1)
    vec[3:4, :] += colsum(gsc)
    vec[4:5, :] += colsum(gz2)
    vec[6:7, :dc] += jnp.sum(gc * cn, axis=0, keepdims=True)


def run_middle(comp, cnt, x, c, ct, gat, att, gp, g2, sm, tb):
    t, d = x.shape
    dc = c.shape[1]
    z = g2.shape[0]
    ff = 2 * d
    dz, cz, fz = d // z, dc // z, ff // z
    sds = jax.ShapeDtypeStruct
    per_copy = t // comp.shape[0] // tb
    w9 = (fz + 5 * dz) // cz
    outs = [
        (d, BF), (d, F32), (dc, F32), (d, BF), (ff, BF), (dc, BF), (d, BF), (d, BF), (ff, BF), (ff, BF),
        (d, BF), (d, BF), (d, BF), (d, BF), (d, BF), (d, BF),
    ]
    return pl.pallas_call(
        functools.partial(middle_kernel, per_copy),
        grid_spec=pltpu.PrefetchScalarGridSpec(
            num_scalar_prefetch=2,
            grid=(t // tb,),
            in_specs=[rows_of(tb, d), rows_of(tb, dc)]
            + [rows_of(tb, d)] * 4
            + [part(z, dz, d, fz // dz + i) for i in range(5)]
            + [part(z, fz, d, 0)]
            + [part(z, cz, d, w9 + i) for i in range(4)]
            + [whole(sm.shape)],
            out_specs=[rows_of(tb, w) for w, _ in outs] + [whole((8, d))],
        ),
        out_shape=[sds((t, w), k) for w, k in outs] + [sds((8, d), F32)],
        compiler_params=params(60),
        cost_estimate=cost(2 * t * (2 * d * d + 8 * d * dc + 6 * d * ff), 60 * MIB),
        name="middle",
    )(comp, cnt, x, c, ct, gat, att, gp, g2, g2, g2, g2, g2, g2, g2, g2, g2, g2, sm)


def last_kernel(dq, dk, dv, dg, x, c, sp, gm, dcp, wq, wk, wv, wg, ws, wh, sm, sg_o, cg_o, gsc_o, gsh_o, vec):
    dc = c.shape[1]
    e = (
        dot_nt(dq[...], flat(wq))
        + dot_nt(dk[...], flat(wk))
        + dot_nt(dv[...], flat(wv))
        + dot_nt(dg[...], flat(wg))
    )
    an, ar = norm(x[...].astype(F32))
    s = sig(sp[...].astype(F32))
    t = e * s
    gsc = (t * an * (1.0 - s)).astype(BF)
    gsh = e.astype(BF)
    gsc_o[...] = gsc
    gsh_o[...] = gsh
    sg_o[...] = gm[...] + norm_back(an, ar, t)
    gc = dot_nt(gsc, flat(ws)) + dot_nt(gsh, flat(wh))
    cn, cr = norm(c[...].astype(F32))
    cg_o[...] = dcp[...] + norm_back(cn, cr, gc * sm[5:6, :dc])

    @pl.when(pl.program_id(0) == 0)
    def _():
        vec[...] = jnp.zeros_like(vec)

    vec[0:1, :] += colsum(gsc)
    vec[1:2, :] += colsum(dq[...])
    vec[5:6, :dc] += jnp.sum(gc * cn, axis=0, keepdims=True)


def run_last(dq, dk, dv, dg, x, c, sp, gm, dcp, g1, sm, tb):
    t, d = x.shape
    dc = c.shape[1]
    z = g1.shape[0]
    dz, cz = d // z, dc // z
    sds = jax.ShapeDtypeStruct
    return pl.pallas_call(
        last_kernel,
        grid=(t // tb,),
        in_specs=[rows_of(tb, d)] * 5
        + [rows_of(tb, dc), rows_of(tb, d), rows_of(tb, d), rows_of(tb, dc)]
        + [part(z, dz, d, i) for i in range(4)]
        + [part(z, cz, d, 4 * dz // cz), part(z, cz, d, 4 * dz // cz + 1), whole(sm.shape)],
        out_specs=[rows_of(tb, d), rows_of(tb, dc), rows_of(tb, d), rows_of(tb, d), whole((8, d))],
        out_shape=[sds((t, d), F32), sds((t, dc), F32), sds((t, d), BF), sds((t, d), BF), sds((8, d), F32)],
        compiler_params=params(60),
        cost_estimate=cost(2 * t * d * (4 * d + 2 * dc), 30 * MIB),
        name="last",
    )(dq, dk, dv, dg, x, c, sp, gm, dcp, g1, g1, g1, g1, g1, g1, sm)


def outer_kernel(a, b, o):
    o[...] = dot_tn(a[...], b[...]).astype(BF)


def outer(a, b):
    t, k = a.shape
    n = b.shape[1]
    kb, nb = min(k, 384), min(n, 768)
    return pl.pallas_call(
        outer_kernel,
        grid=(k // kb, n // nb),
        in_specs=[
            pl.BlockSpec((t, kb), lambda i, j: (0, i)),
            pl.BlockSpec((t, nb), lambda i, j: (0, j)),
        ],
        out_specs=pl.BlockSpec((kb, nb), lambda i, j: (i, j)),
        out_shape=jax.ShapeDtypeStruct((k, n), BF),
        compiler_params=params(60),
        cost_estimate=cost(2 * t * k * n, 2 * (t * k + t * n + k * n)),
        name="outer",
    )(a, b)


def split_rows(w, z):
    return w.reshape(z, w.shape[0] // z, w.shape[1])


def body(ndp, nfs, *args):
    (single, condition, pair_tensor, counts, complex_of, cotangent, condition_gain, scale_weight, scale_bias,
     shift_weight, query_weight, query_bias, key_weight, value_weight, gate_weight, output_weight, pair_gain,
     pair_weight, branch_gate_weight, branch_gate_bias, transition_gain, transition_scale_weight,
     transition_scale_bias, transition_shift_weight, hidden_gate, hidden_value, hidden_output, final_gate_weight,
     final_gate_bias) = args
    copies, rows, d = single.shape
    dc = condition.shape[2]
    t = copies * rows
    heads = pair_weight.shape[1]
    ncomp = counts.shape[0]
    dz = d // nfs
    x = single.reshape(t, d)
    c = condition.reshape(t, dc)
    ct = cotangent.reshape(t, d)
    me = lax.axis_index(DP)
    unit = 16 * ndp

    def padded(total):
        return -(-total // unit) * unit

    def row(v):
        return jnp.pad(v, (0, d - v.shape[0]))[None, :]

    vectors = (scale_bias, query_bias, branch_gate_bias, transition_scale_bias, final_gate_bias,
               condition_gain, transition_gain)
    small = jnp.concatenate([row(v) for v in vectors] + [jnp.zeros((1, d), BF)], axis=0)
    rows1 = 4 * dz + 2 * scale_weight.shape[0]
    pack1 = jnp.concatenate(
        [query_weight, key_weight, value_weight, gate_weight, scale_weight, shift_weight, small], axis=0
    )
    size1 = padded(rows1 + 8)
    pack1 = jnp.pad(pack1, ((0, size1 - pack1.shape[0]), (0, 0)))
    pack2 = jnp.concatenate(
        [hidden_output, output_weight, hidden_gate[:, :d], hidden_gate[:, d:], hidden_value[:, :d],
         hidden_value[:, d:], branch_gate_weight, transition_scale_weight, transition_shift_weight,
         final_gate_weight], axis=0
    )
    rows2 = pack2.shape[0]
    size2 = padded(rows2)
    pack2 = jnp.pad(pack2, ((0, size2 - rows2), (0, 0)))

    def gather(pack):
        n = pack.shape[0] // ndp
        mine = lax.dynamic_slice_in_dim(pack, me * n, n, axis=0)
        return lax.all_gather(mine, (FS, DP), axis=0, tiled=True).reshape(nfs, pack.shape[0], d)

    g1 = gather(pack1)
    g2 = gather(pack2)
    pgain = lax.all_gather(pair_gain, FS, axis=0, tiled=True).astype(F32)
    pw = lax.all_gather(pair_weight, FS, axis=0, tiled=True)
    sm = jnp.transpose(g1[:, rows1 : rows1 + 8, :dz], (1, 0, 2)).reshape(8, d).astype(F32)
    cz = dc // nfs
    gains = jnp.transpose(g1[:, rows1 + 5 : rows1 + 7, :cz], (1, 0, 2)).reshape(2, dc).astype(F32)
    sm = jnp.concatenate([sm[:5], jnp.pad(gains, ((0, 0), (0, d - dc))), sm[7:]], axis=0)

    pair_float = pair_tensor.astype(F32)
    pair_norm, pair_rstd = norm(pair_float)
    pair_low = (pair_norm * pgain).astype(BF)
    bias_local = jnp.transpose(dot(pair_low, pw).astype(BF), (0, 3, 1, 2))
    bias = lax.all_gather(bias_local, FS, axis=3, tiled=True)
    bias = lax.all_gather(bias, DP, axis=2, tiled=True)

    first_in, q, k, v, gp, sp, cl1 = run_first(x, c, g1, sm, rows)
    p, att, gated = run_attend(complex_of, counts, q, k, v, gp, bias, 2)
    (out, gm, dcp, si, act, cl2, gt2, gz2, gh, gv, gsc2, gsh2, gt1, gz1, da, dg, vec_a) = run_middle(
        complex_of, counts, x, c, ct, gated, att, gp, g2, sm, rows // 2
    )
    dq, dk, dv, db = run_attend_back(complex_of, p, q, k, v, da, att, ncomp, 2)
    sgrad, cgrad, gsc1, gsh1, vec_b = run_last(dq, dk, dv, dg, x, c, sp, gm, dcp, g1, sm, rows)

    w_hg = outer(si, gh)
    w_hv = outer(si, gv)
    grads2 = [outer(act, gt2), outer(gated, gt1), w_hg[:, :d], w_hg[:, d:], w_hv[:, :d], w_hv[:, d:],
              outer(c, gz1), outer(cl2, gsc2), outer(cl2, gsh2), outer(c, gz2)]
    pg2 = jnp.concatenate([split_rows(w, nfs) for w in grads2], axis=1)
    pg2 = jnp.pad(pg2, ((0, 0), (0, size2 - rows2), (0, 0)))

    def reduce(pack):
        n = pack.shape[1] // ndp
        part_sum = lax.psum_scatter(
            pack.reshape(nfs * pack.shape[1], d), (FS, DP), scatter_dimension=0, tiled=True
        )
        return lax.all_gather(part_sum, DP, axis=0, tiled=True).astype(F32)

    r2 = reduce(pg2)

    partial_rows = lax.psum_scatter(db, DP, scatter_dimension=2, tiled=True)
    bias_grad = lax.psum_scatter(partial_rows, FS, scatter_dimension=3, tiled=True)
    bias_grad = jnp.transpose(bias_grad, (0, 2, 3, 1))
    pair_width = pair_low.shape[3]
    pw_grad = dot_tn(pair_low.reshape(-1, pair_width), bias_grad.reshape(-1, heads))
    grad_low = dot(bias_grad, pw.T)
    pgain_grad = jnp.sum(grad_low * pair_norm, axis=(0, 1, 2))
    pair_grad = norm_back(pair_norm, pair_rstd, grad_low * pgain)

    vec = (vec_a + vec_b).astype(BF)
    vz = jnp.transpose(vec.reshape(8, nfs, dz), (1, 0, 2))
    cv = jnp.transpose(vec[5:7, :dc].reshape(2, nfs, cz), (1, 0, 2))
    vz = jnp.concatenate(
        [vz[:, :5], jnp.pad(cv, ((0, 0), (0, 0), (0, dz - cz))), jnp.zeros((nfs, 1, dz), BF)], axis=1
    )
    small_grad = jnp.pad(vz, ((0, 0), (0, 0), (0, d - dz)))
    pgz = jnp.pad(pgain_grad.astype(BF).reshape(nfs, 1, -1), ((0, 0), (0, 0), (0, d - pair_width // nfs)))
    pwz = jnp.pad(pw_grad.astype(BF).reshape(nfs, 1, -1), ((0, 0), (0, 0), (0, d - pair_width * heads // nfs)))
    grads1 = [outer(first_in, dq), outer(first_in, dk), outer(first_in, dv), outer(first_in, dg),
              outer(cl1, gsc1), outer(cl1, gsh1)]
    pg1 = jnp.concatenate([split_rows(w, nfs) for w in grads1] + [small_grad, pgz, pwz], axis=1)
    pg1 = jnp.pad(pg1, ((0, 0), (0, size1 - pg1.shape[1]), (0, 0)))
    r1 = reduce(pg1)

    def take(r, at, n):
        return r[at : at + n]

    fz = hidden_output.shape[0]
    o1 = [take(r1, i * dz, dz) for i in range(4)]
    s1 = [take(r1, 4 * dz + i * cz, cz) for i in range(2)]
    sv = r1[rows1 : rows1 + 8]
    ext = r1[rows1 + 8 : rows1 + 10]
    at = fz + 5 * dz
    o2 = [take(r2, fz + i * dz, dz) for i in range(5)]
    c2 = [take(r2, at + i * cz, cz) for i in range(4)]
    shape3 = (copies, rows, d)
    return (
        out.reshape(shape3),
        sgrad.reshape(shape3),
        cgrad.reshape(copies, rows, dc),
        pair_grad,
        sv[5, :cz],
        s1[0],
        sv[0, :dz],
        s1[1],
        o1[0],
        sv[1, :dz],
        o1[1],
        o1[2],
        o1[3],
        o2[0],
        ext[0, : pair_width // nfs],
        ext[1, : pair_width * heads // nfs].reshape(pair_width // nfs, heads),
        c2[0],
        sv[2, :dz],
        sv[6, :cz],
        c2[1],
        sv[3, :dz],
        c2[2],
        jnp.concatenate([o2[1], o2[2]], axis=1),
        jnp.concatenate([o2[3], o2[4]], axis=1),
        take(r2, 0, fz),
        c2[3],
        sv[4, :dz],
    )


def solution(mesh):
    both = (DP, FS)
    wide = P(both, None, None)
    mat = P(FS, None)
    vec = P(FS)
    pair = P(None, DP, FS, None)
    weights = (vec, mat, vec, mat, mat, vec, mat, mat, mat, mat, vec, mat, mat, vec, vec, mat, vec, mat, mat, mat,
               mat, mat, vec)
    in_specs = (wide, wide, pair, P(), P(both), wide) + weights
    out_specs = (wide, wide, wide, pair) + weights
    run = functools.partial(body, mesh.shape[DP], mesh.shape[FS])
    return jax.shard_map(run, mesh=mesh, in_specs=in_specs, out_specs=out_specs, check_vma=False)
```

```python
import functools

import jax
import jax.numpy as jnp
from jax import lax
from jax.experimental import pallas as pl
from jax.experimental.pallas import tpu as pltpu
from jax.sharding import PartitionSpec as P

BF = jnp.bfloat16
F32 = jnp.float32
EPSILON = 1e-05
DP = "dp"
FS = "fsdp"
MIB = 1024 * 1024
NEGATIVE = -1000000000.0


def norm(v):
    c = v - jnp.mean(v, axis=-1, keepdims=True)
    r = lax.rsqrt(jnp.mean(c * c, axis=-1, keepdims=True) + EPSILON)
    return c * r, r


def norm_back(n, r, u):
    return r * (u - jnp.mean(u, axis=-1, keepdims=True) - n * jnp.mean(u * n, axis=-1, keepdims=True))


def sig(v):
    return 0.5 * jnp.tanh(0.5 * v) + 0.5


def dot(a, b):
    return jnp.dot(a, b, preferred_element_type=F32)


def dot_nt(a, b):
    return lax.dot_general(a, b, (((1,), (1,)), ((), ())), preferred_element_type=F32)


def dot_tn(a, b):
    return lax.dot_general(a, b, (((0,), (0,)), ((), ())), preferred_element_type=F32)


def flat(ref):
    v = ref[...]
    return v.reshape(v.shape[0] * v.shape[1], v.shape[2])


def colsum(v):
    return jnp.sum(v.astype(F32), axis=0, keepdims=True)


def first_kernel(x, c, wq, wk, wv, wg, ws, wh, sm, fi, q, k, v, gp, sp, cl):
    cn, _ = norm(c[...].astype(F32))
    low = (cn * sm[5:6, : cn.shape[1]]).astype(BF)
    cl[...] = low
    pre = dot(low, flat(ws)) + sm[0:1, :]
    shift = dot(low, flat(wh))
    sp[...] = pre.astype(BF)
    an, _ = norm(x[...].astype(F32))
    first = (sig(pre) * an + shift).astype(BF)
    fi[...] = first
    q[...] = (dot(first, flat(wq)) + sm[1:2, :]).astype(BF)
    k[...] = dot(first, flat(wk)).astype(BF)
    v[...] = dot(first, flat(wv)).astype(BF)
    gp[...] = dot(first, flat(wg)).astype(BF)


def whole(shape):
    return pl.BlockSpec(shape, lambda *i: (0,) * len(shape), pipeline_mode=pl.Buffered(1))


def part(z, rows, width, at):
    return pl.BlockSpec((z, rows, width), lambda *i: (0, at, 0), pipeline_mode=pl.Buffered(1))


def rows_of(tb, width):
    return pl.BlockSpec((tb, width), lambda i, *_: (i, 0))


def params(limit, **kw):
    return pltpu.CompilerParams(vmem_limit_bytes=limit * MIB, **kw)


def cost(flops, nbytes, trans=0):
    return pl.CostEstimate(flops=int(flops), bytes_accessed=int(nbytes), transcendentals=int(trans))


def run_first(x, c, g1, sm, tb):
    t, d = x.shape
    dc = c.shape[1]
    z = g1.shape[0]
    dz, cz = d // z, dc // z
    sds = jax.ShapeDtypeStruct
    return pl.pallas_call(
        first_kernel,
        grid=(t // tb,),
        in_specs=[rows_of(tb, d), rows_of(tb, dc)]
        + [part(z, dz, d, i) for i in range(4)]
        + [part(z, cz, d, 4 * dz // cz), part(z, cz, d, 4 * dz // cz + 1), whole(sm.shape)],
        out_specs=[rows_of(tb, d)] * 6 + [rows_of(tb, dc)],
        out_shape=[sds((t, d), BF)] * 6 + [sds((t, dc), BF)],
        compiler_params=params(60),
        cost_estimate=cost(2 * t * d * (4 * d + 2 * dc), 20 * MIB),
        name="first",
    )(x, c, g1, g1, g1, g1, g1, g1, sm)


def windows(per, hs):
    out = []
    for j in range(per):
        lo = j * hs
        w = min(lo // 128 * 128, max(per * hs - 256, 0))
        out.append((w, lo - w))
    return out


def lane_mask(o, hs, width):
    lane = lax.broadcasted_iota(jnp.int32, (1, width), 1)
    return jnp.where((lane >= o) & (lane < o + hs), 1.0, 0.0).astype(BF)


def put(acc, w, width, val):
    for b in range(width // 128):
        key = w // 128 + b
        piece = val[:, 128 * b : 128 * b + 128]
        acc[key] = piece if key not in acc else acc[key] + piece


def attend_body(per, hs, limit, q, k, v, bias_of, gp, keep, att, gated):
    width = min(256, per * hs)
    mrow = jnp.where(
        lax.broadcasted_iota(jnp.int32, (1, k.shape[0]), 1) < limit, 0.0, NEGATIVE
    ).astype(F32)
    scale = hs ** (-0.5)
    acc = {}
    for j, (w, o) in enumerate(windows(per, hs)):
        m = lane_mask(o, hs, width)
        s = dot_nt(q[:, w : w + width] * m, k[:, w : w + width]) * scale
        s = s + (bias_of(j).astype(F32) + mrow)
        e = jnp.exp(s - jnp.max(s, axis=-1, keepdims=True))
        pb = (e * (1.0 / jnp.sum(e, axis=-1, keepdims=True))).astype(BF)
        keep(j, pb)
        put(acc, w, width, dot(pb, v[:, w : w + width] * m))
    for key, val in acc.items():
        cols = slice(128 * key, 128 * key + 128)
        att[:, cols] = val.astype(BF)
        gated[:, cols] = (sig(gp[:, cols].astype(F32)) * val).astype(BF)


def attend_kernel(per, hs, comp, cnt, q, k, v, b, gp, p_out, att, gated):
    def keep(j, val):
        p_out[0, j] = val

    limit = cnt[comp[pl.program_id(0)]]
    attend_body(per, hs, limit, q, k, v, lambda j: b[0, j], gp, keep, att, gated)


def run_attend(comp, cnt, q, k, v, gp, bias, groups):
    copies = comp.shape[0]
    t, d = q.shape
    rows = t // copies
    heads = bias.shape[1]
    per, dg = heads // groups, d // groups
    blk = pl.BlockSpec((rows, dg), lambda c, g, *_: (c, g))
    sds = jax.ShapeDtypeStruct
    return pl.pallas_call(
        functools.partial(attend_kernel, per, d // heads),
        grid_spec=pltpu.PrefetchScalarGridSpec(
            num_scalar_prefetch=2,
            grid=(copies, groups),
            in_specs=[
                blk,
                blk,
                blk,
                pl.BlockSpec((1, per, rows, rows), lambda c, g, comp, cnt: (comp[c], g, 0, 0)),
                blk,
            ],
            out_specs=[
                pl.BlockSpec((1, per, rows, rows), lambda c, g, *_: (c, g, 0, 0)),
                blk,
                blk,
            ],
        ),
        out_shape=[sds((copies, heads, rows, rows), BF), sds((t, d), BF), sds((t, d), BF)],
        compiler_params=params(60),
        cost_estimate=cost(2 * 2 * t * rows * heads * 256, 40 * MIB, t * rows * heads),
        name="attend",
    )(comp, cnt, q, k, v, bias, gp)


def attend_back_kernel(per, hs, comp, p, q, k, v, da, at, dq, dk, dv, db, acc):
    c = pl.program_id(1)
    last = pl.num_programs(1) - 1
    n = comp[c]
    width = min(256, per * hs)
    scale = hs ** (-0.5)

    @pl.when(c == 0)
    def _():
        acc[...] = jnp.zeros_like(acc)

    aq, ak, av = {}, {}, {}
    prod = da[...].astype(F32) * at[...].astype(F32)
    lane = lax.broadcasted_iota(jnp.int32, (1, per * hs), 1)
    for j, (w, o) in enumerate(windows(per, hs)):
        m = lane_mask(o, hs, width)
        lo = w + o
        inside = (lane >= lo) & (lane < lo + hs)
        delta = jnp.sum(jnp.where(inside, prod, 0.0), axis=-1, keepdims=True)
        pj = p[0, j]
        win = slice(w, w + width)
        dam = da[:, win] * m
        dp = dot_nt(dam, v[:, win])
        ds = pj.astype(F32) * (dp - delta)
        acc[n, j] += ds
        dsb = ds.astype(BF)
        put(av, w, width, dot_tn(pj, dam))
        put(aq, w, width, dot(dsb, k[:, win] * m))
        put(ak, w, width, dot_tn(dsb, q[:, win] * m))
    for key in aq:
        cols = slice(128 * key, 128 * key + 128)
        dq[:, cols] = (aq[key] * scale).astype(BF)
        dk[:, cols] = (ak[key] * scale).astype(BF)
        dv[:, cols] = av[key].astype(BF)

    @pl.when(c == last)
    def _():
        db[...] = acc[...].astype(BF)


def run_attend_back(comp, p, q, k, v, da, att, ncomp, groups):
    copies, heads, rows, _ = p.shape
    t, d = q.shape
    per, dg = heads // groups, d // groups
    blk = pl.BlockSpec((rows, dg), lambda g, c, *_: (c, g))
    sds = jax.ShapeDtypeStruct
    return pl.pallas_call(
        functools.partial(attend_back_kernel, per, d // heads),
        grid_spec=pltpu.PrefetchScalarGridSpec(
            num_scalar_prefetch=1,
            grid=(groups, copies),
            in_specs=[pl.BlockSpec((1, per, rows, rows), lambda g, c, *_: (c, g, 0, 0))]
            + [blk] * 5,
            out_specs=[blk] * 3
            + [
                pl.BlockSpec(
                    (ncomp, per, rows, rows),
                    lambda g, c, *_: (0, g, 0, 0),
                    pipeline_mode=pl.Buffered(1),
                )
            ],
            scratch_shapes=[pltpu.VMEM((ncomp, per, rows, rows), F32)],
        ),
        out_shape=[sds((t, d), BF)] * 3 + [sds((ncomp, heads, rows, rows), BF)],
        compiler_params=params(60),
        cost_estimate=cost(4 * 2 * t * rows * heads * 256, 40 * MIB),
        name="attend_back",
    )(comp, p, q, k, v, da, att)


def middle_kernel(per_copy, comp, cnt, x, c, ct, gat, att, gp, wo, hl, hr, vl, vr, ho, bg, ts, th, fg, sm,
                  out, gm_o, dc_o, si_o, act_o, cl_o, g2_o, gz2_o, gh_o, gv_o, gsc_o, gsh_o, g1_o, gz1_o, da_o, dg_o, vec):
    i = pl.program_id(0)
    tb, d = x.shape
    dc = c.shape[1]
    copy = i // per_copy
    limit = cnt[comp[copy]] - (i % per_copy) * tb
    keep = jnp.where(lax.broadcasted_iota(jnp.int32, (tb, 1), 0) < limit, 1.0, 0.0).astype(F32)

    low = c[...]
    y1 = dot(gat[...], flat(wo))
    z1 = sig(dot(low, flat(bg)) + sm[2:3, :])
    kz1 = keep * z1
    mid = x[...].astype(F32) + kz1 * y1
    cn, cr = norm(low.astype(F32))
    gain = sm[6:7, :dc]
    cl = (cn * gain).astype(BF)
    cl_o[...] = cl
    s2 = sig(dot(cl, flat(ts)) + sm[3:4, :])
    mn, mr = norm(mid)
    si = (s2 * mn + dot(cl, flat(th))).astype(BF)
    si_o[...] = si
    zh = ho.shape[0] // 2
    kept = []
    y2 = None
    for half, (hg, hv) in enumerate(((hl, vl), (hr, vr))):
        u = dot(si, flat(hg))
        w = dot(si, flat(hv))
        su = sig(u)
        silu = u * su
        act = (silu * w).astype(BF)
        act_o[:, half * d : half * d + d] = act
        kept.append((w * su * (1.0 + u - silu), silu))
        hov = ho[half * zh : half * zh + zh]
        term = dot(act, hov.reshape(d, d))
        y2 = term if y2 is None else y2 + term
    z2 = sig(dot(low, flat(fg)) + sm[4:5, :])
    g = ct[...].astype(F32)
    kz2 = keep * z2
    out[...] = (mid + kz2 * y2).astype(BF)
    gk = g * kz2
    g2 = gk.astype(BF)
    gz2 = (gk * y2 * (1.0 - z2)).astype(BF)
    g2_o[...] = g2
    gz2_o[...] = gz2
    e = None
    for half, (hg, hv) in enumerate(((hl, vl), (hr, vr))):
        hov = ho[half * zh : half * zh + zh]
        ga = dot_nt(g2, hov.reshape(d, d))
        du, silu = kept[half]
        gh = (ga * du).astype(BF)
        gv = (ga * silu).astype(BF)
        gh_o[:, half * d : half * d + d] = gh
        gv_o[:, half * d : half * d + d] = gv
        term = dot_nt(gh, flat(hg)) + dot_nt(gv, flat(hv))
        e = term if e is None else e + term
    t = e * s2
    gsc = (t * mn * (1.0 - s2)).astype(BF)
    gsh = e.astype(BF)
    gsc_o[...] = gsc
    gsh_o[...] = gsh
    gc = dot_nt(gsc, flat(ts)) + dot_nt(gsh, flat(th))
    gm = g + norm_back(mn, mr, t)
    gm_o[...] = gm
    kz = gm * kz1
    g1 = kz.astype(BF)
    gz1 = (kz * y1 * (1.0 - z1)).astype(BF)
    g1_o[...] = g1
    gz1_o[...] = gz1
    dc_o[...] = norm_back(cn, cr, gc * gain) + dot_nt(gz2, flat(fg)) + dot_nt(gz1, flat(bg))
    gg = dot_nt(g1, flat(wo))
    sp = sig(gp[...].astype(F32))
    da = gg * sp
    da_o[...] = da.astype(BF)
    dg_o[...] = (da * att[...].astype(F32) * (1.0 - sp)).astype(BF)

    @pl.when(i == 0)
    def _():
        vec[...] = jnp.zeros_like(vec)

    vec[2:3, :] += colsum(gz1)
    vec[3:4, :] += colsum(gsc)
    vec[4:5, :] += colsum(gz2)
    vec[6:7, :dc] += jnp.sum(gc * cn, axis=0, keepdims=True)


def run_middle(comp, cnt, x, c, ct, gat, att, gp, g2, sm, tb):
    t, d = x.shape
    dc = c.shape[1]
    z = g2.shape[0]
    ff = 2 * d
    dz, cz, fz = d // z, dc // z, ff // z
    sds = jax.ShapeDtypeStruct
    per_copy = t // comp.shape[0] // tb
    w9 = (fz + 5 * dz) // cz
    outs = [
        (d, BF), (d, F32), (dc, F32), (d, BF), (ff, BF), (dc, BF), (d, BF), (d, BF), (ff, BF), (ff, BF),
        (d, BF), (d, BF), (d, BF), (d, BF), (d, BF), (d, BF),
    ]
    return pl.pallas_call(
        functools.partial(middle_kernel, per_copy),
        grid_spec=pltpu.PrefetchScalarGridSpec(
            num_scalar_prefetch=2,
            grid=(t // tb,),
            in_specs=[rows_of(tb, d), rows_of(tb, dc)]
            + [rows_of(tb, d)] * 4
            + [part(z, dz, d, fz // dz + i) for i in range(5)]
            + [part(z, fz, d, 0)]
            + [part(z, cz, d, w9 + i) for i in range(4)]
            + [whole(sm.shape)],
            out_specs=[rows_of(tb, w) for w, _ in outs] + [whole((8, d))],
        ),
        out_shape=[sds((t, w), k) for w, k in outs] + [sds((8, d), F32)],
        compiler_params=params(60),
        cost_estimate=cost(2 * t * (2 * d * d + 8 * d * dc + 6 * d * ff), 60 * MIB),
        name="middle",
    )(comp, cnt, x, c, ct, gat, att, gp, g2, g2, g2, g2, g2, g2, g2, g2, g2, g2, sm)


def last_body(dq, dk, dv, dg, x, c, sp, gm, dcp, wq, wk, wv, wg, ws, wh, sm, sg_o, cg_o, gsc_o, gsh_o, vec):
    dc = c.shape[1]
    e = (
        dot_nt(dq[...], flat(wq))
        + dot_nt(dk[...], flat(wk))
        + dot_nt(dv[...], flat(wv))
        + dot_nt(dg[...], flat(wg))
    )
    an, ar = norm(x[...].astype(F32))
    s = sig(sp[...].astype(F32))
    t = e * s
    gsc = (t * an * (1.0 - s)).astype(BF)
    gsh = e.astype(BF)
    gsc_o[...] = gsc
    gsh_o[...] = gsh
    sg_o[...] = gm[...] + norm_back(an, ar, t)
    gc = dot_nt(gsc, flat(ws)) + dot_nt(gsh, flat(wh))
    cn, cr = norm(c[...].astype(F32))
    cg_o[...] = dcp[...] + norm_back(cn, cr, gc * sm[5:6, :dc])
    vec[0:1, :] += colsum(gsc)
    vec[1:2, :] += colsum(dq[...])
    vec[5:6, :dc] += jnp.sum(gc * cn, axis=0, keepdims=True)


def last_kernel(*refs):
    @pl.when(pl.program_id(0) == 0)
    def _():
        refs[-1][...] = jnp.zeros_like(refs[-1])

    last_body(*refs)


def run_last(dq, dk, dv, dg, x, c, sp, gm, dcp, g1, sm, tb):
    t, d = x.shape
    dc = c.shape[1]
    z = g1.shape[0]
    dz, cz = d // z, dc // z
    sds = jax.ShapeDtypeStruct
    return pl.pallas_call(
        last_kernel,
        grid=(t // tb,),
        in_specs=[rows_of(tb, d)] * 5
        + [rows_of(tb, dc), rows_of(tb, d), rows_of(tb, d), rows_of(tb, dc)]
        + [part(z, dz, d, i) for i in range(4)]
        + [part(z, cz, d, 4 * dz // cz), part(z, cz, d, 4 * dz // cz + 1), whole(sm.shape)],
        out_specs=[rows_of(tb, d), rows_of(tb, dc), rows_of(tb, d), rows_of(tb, d), whole((8, d))],
        out_shape=[sds((t, d), F32), sds((t, dc), F32), sds((t, d), BF), sds((t, d), BF), sds((8, d), F32)],
        compiler_params=params(60),
        cost_estimate=cost(2 * t * d * (4 * d + 2 * dc), 30 * MIB),
        name="last",
    )(dq, dk, dv, dg, x, c, sp, gm, dcp, g1, g1, g1, g1, g1, g1, sm)


def flip(i, b):
    return i + b * (1 - 2 * ((i // b) % 2))


def flips(i, bs):
    for b in bs:
        i = flip(i, b)
    return i


def subsets(bs):
    out = [()]
    for b in bs:
        out = out + [s + (b,) for s in out]
    return out


def bits_of(n):
    out, b = [], 1
    while b < n:
        out.append(b)
        b *= 2
    return out


def peers(ndp, nfs):
    return nfs - 1 + len(bits_of(ndp))


class Plan:
    def __init__(self, ndp, nfs, send, recv, local):
        self.ndp, self.nfs, self.send, self.recv, self.lsem = ndp, nfs, send, recv, local
        self.dp, self.z = lax.axis_index(DP), lax.axis_index(FS)
        self.sent, self.locals = [], 0

    def barrier(self):
        sem = pltpu.get_barrier_semaphore()
        to = [(self.dp, (self.z + k) % self.nfs) for k in range(1, self.nfs)]
        to += [(flip(self.dp, b), self.z) for b in bits_of(self.ndp)]
        for dev in to:
            pl.semaphore_signal(sem, inc=1, device_id=dev, device_id_type=pl.DeviceIdType.MESH)
        pl.semaphore_wait(sem, len(to))

    def copy(self, src, dst, dp, z):
        n = len(self.sent)
        c = pltpu.make_async_remote_copy(
            src_ref=src, dst_ref=dst, send_sem=self.send.at[n], recv_sem=self.recv.at[n], device_id=(dp, z),
            device_id_type=pl.DeviceIdType.MESH,
        )
        self.sent.append(c)
        return c

    def here(self, src, dst):
        self.locals += 1
        return pltpu.make_async_copy(src, dst, self.lsem.at[self.locals - 1])

    def finish(self):
        for c in self.sent:
            c.wait_send()


def start(cs):
    for c in cs:
        c.start()


def arrive(cs):
    for c in cs:
        c.wait_recv()


def spread(plan, halves, slot, own, first, extra):
    k = len(halves[0][1])
    chips, sibs = [], []
    fresh = [(part_, ()) for part_, _ in halves]
    for s in range(k + 1):
        sibs.append([])
        for part_, sub in fresh:
            e = flips(plan.dp, sub)
            src = slot(part_, e) if sub else own(part_)
            sibs[-1].append(plan.copy(src, slot(part_, e), flip(plan.dp, 1), plan.z))
        if s == k:
            break
        chips.append([])
        for part_, order in halves:
            for sub in subsets(order[:s]):
                e = flips(plan.dp, sub)
                src = slot(part_, e) if sub else own(part_)
                chips[-1].append(plan.copy(src, slot(part_, e), flip(plan.dp, order[s]), plan.z))
        fresh = [(p_, sub + (order[s],)) for p_, order in halves for sub in subsets(order[:s])]

    def opening():
        first()
        if k:
            start(chips[0])
        start(sibs[0])

    def middle(s):
        def step():
            arrive(chips[s - 1])
            if s < k:
                start(chips[s])
            start(sibs[s])

        return step

    def closing():
        for group in sibs:
            arrive(group)
        extra()

    return [opening] + [middle(s) for s in range(1, k + 1)] + [closing]


def two_orders(ndp):
    bs = [2 * b for b in bits_of(ndp // 2)]
    return bs, bs[::-1]


def gather_steps(plan, shard, g, ready):
    nfs, n = plan.nfs, g.shape[1] // plan.ndp
    mine = shard.at[pl.ds(plan.dp * n, n), :]
    here = g.at[plan.z, pl.ds(plan.dp * n, n), :]
    own = plan.here(mine, here)
    zs = [plan.copy(mine, here, plan.dp, (plan.z + k) % nfs) for k in range(1, nfs)]
    hz = nfs // 2
    up, down = two_orders(plan.ndp)
    halves = [(pl.ds(0, hz), up), (pl.ds(hz, nfs - hz), down)]

    def slot(part_, e):
        return g.at[part_, pl.ds(e * n, n), :]

    def begin():
        ready()
        start(zs)
        own.start()

    def landed():
        own.wait()
        arrive(zs)

    rest = spread(plan, halves, slot, lambda p_: slot(p_, plan.dp), landed, lambda: None)
    return [begin] + rest


def place(cw, full, at, rows_first):
    a = lax.broadcasted_iota(jnp.int32, (cw, full) if rows_first else (full, cw), 0)
    b = lax.broadcasted_iota(jnp.int32, (cw, full) if rows_first else (full, cw), 1)
    hit = b == a + at if rows_first else a == b + at
    return jnp.where(hit, 1.0, 0.0).astype(BF)


def bias_gather_steps(plan, bl, zb, bias):
    nfs = plan.nfs
    nh, r, cw = bl.shape
    full = cw * nfs
    own = plan.here(bl, zb.at[plan.z])
    mine = pl.ds(pl.multiple_of(plan.dp * r, r), r)
    zs = [plan.copy(bl, zb.at[plan.z], plan.dp, (plan.z + k) % nfs) for k in range(1, nfs)]
    up, down = two_orders(plan.ndp)
    hh = nh // 2
    halves = [(pl.ds(0, hh), up), (pl.ds(hh, nh - hh), down)]

    def begin():
        own.start()
        start(zs)

    def join():
        own.wait()
        arrive(zs)

        def some(i, carry):
            total = None
            for zz in range(nfs):
                v = zb[zz, pl.ds(i * 8, 8)].reshape(8 * r, cw)
                term = dot(v, place(cw, full, zz * cw, True))
                total = term if total is None else total + term
            bias[pl.ds(i * 8, 8), mine, :] = total.astype(BF).reshape(8, r, full)
            return carry

        lax.fori_loop(0, nh // 8, some, 0)

    def slot(p_, e):
        return bias.at[p_, pl.ds(e * r, r), :]

    rest = spread(plan, halves, slot, lambda p_: slot(p_, plan.dp), join, lambda: None)
    return [begin] + rest


def add_rows(dst, src):
    def one(i, carry):
        dst[i] = dst[i] + src[i]
        return carry

    lax.fori_loop(0, dst.shape[0], one, 0)


def sum_steps(plan, piece, acc, crecv, rbuf, cut, ready):
    nchip = acc.shape[0]
    dp, z = plan.dp, plan.z
    m, core = dp // 2, dp % 2
    cs = [plan.copy(piece(2 * f + 1 - core), crecv.at[f], flip(dp, 1), z) for f in range(nchip)]
    ls = [plan.here(piece(2 * f + core), acc.at[f]) for f in range(nchip)]
    bs = bits_of(nchip)
    orders = (bs, bs[::-1])
    rounds = []
    at = [0, 0]
    for s in range(len(bs)):
        rounds.append([])
        for h, order in enumerate(orders):
            part_ = pl.ds(*cut[h])
            for sub in subsets(order[s + 1 :]):
                f = flips(m, (order[s],) + sub)
                c = plan.copy(acc.at[f, part_], rbuf.at[at[h], part_], flip(dp, 2 * order[s]), z)
                rounds[-1].append((c, flips(m, sub), at[h], part_))
                at[h] += 1

    def begin():
        ready()
        start(cs)
        start(ls)

    def pair():
        for f in range(nchip):
            ls[f].wait()
            cs[f].wait_recv()
            add_rows(acc.at[f], crecv.at[f])
        if rounds:
            start([c[0] for c in rounds[0]])

    def chip(s):
        def step():
            for c, f, o, part_ in rounds[s - 1]:
                c.wait_recv()
                add_rows(acc.at[f, part_], rbuf.at[o, part_])
            if s < len(bs):
                start([c[0] for c in rounds[s]])

        return step

    return [begin, pair] + [chip(s) for s in range(1, len(bs) + 1)]


def join_steps(one, two):
    def both():
        one[-1]()
        two[0]()

    return one[:-1] + [both] + two[1:]


def reduce_steps(plan, pg, out, acc, crecv, rbuf, zr, fin, ready):
    nfs, n = plan.nfs, acc.shape[2]
    dp, z = plan.dp, plan.z
    hz = nfs // 2
    sums = sum_steps(plan, lambda e: pg.at[:, pl.ds(e * n, n), :], acc, crecv, rbuf, ((0, hz), (hz, nfs - hz)), ready)
    zs = [plan.copy(acc.at[dp // 2, (z + k) % nfs], zr.at[k - 1], dp, (z + k) % nfs) for k in range(1, nfs)]
    keep = plan.here(fin, out.at[pl.ds(dp * n, n), :])
    w = fin.shape[1] // 2
    up, down = two_orders(plan.ndp)
    halves = [(pl.ds(0, w), up), (pl.ds(w, w), down)]

    def total():
        arrive(zs)
        t = acc[dp // 2, z].astype(F32)
        for k in range(nfs - 1):
            t = t + zr[k].astype(F32)
        fin[...] = t.astype(BF)
        keep.start()

    rest = spread(plan, halves, lambda p_, e: out.at[pl.ds(e * n, n), p_], lambda p_: fin.at[:, p_], total, keep.wait)
    return join_steps(sums, [lambda: start(zs)]) + rest


def bias_reduce_steps(plan, db, out, acc, crecv, rbuf, zs, zr):
    nfs = plan.nfs
    dp, z = plan.dp, plan.z
    nchip, nh, r, full = acc.shape
    cw = full // nfs
    hh = nh // 2
    sums = sum_steps(plan, lambda e: db.at[:, pl.ds(e * r, r), :], acc, crecv, rbuf, ((0, hh), (hh, nh - hh)), lambda: None)
    to = [plan.copy(zs.at[(z + k) % nfs], zr.at[k - 1], dp, (z + k) % nfs) for k in range(1, nfs)]

    def cut():
        def some(i, carry):
            v = acc[dp // 2, pl.ds(i * 8, 8)].reshape(8 * r, full)
            for zz in range(nfs):
                zs[zz, pl.ds(i * 8, 8)] = dot(v, place(cw, full, zz * cw, False)).astype(BF).reshape(8, r, cw)
            return carry

        lax.fori_loop(0, nh // 8, some, 0)
        start(to)

    def total():
        arrive(to)

        def one(i, carry):
            t = zs[z, i].astype(F32)
            for k in range(nfs - 1):
                t = t + zr[k, i].astype(F32)
            out[i] = t.astype(BF).astype(F32)
            return carry

        lax.fori_loop(0, nh, one, 0)

    return join_steps(sums, [cut]) + [total]


DMA = pltpu.SemaphoreType.DMA


def pair_params(tg):
    m = tg[...].reshape(128, 128)
    rows = dot_tn(m, place(128, 128, 0, True))
    return rows[0:16].astype(BF), rows[16:17]


def pair_rows(pair, n, i):
    x = pair[n, pl.ds(i * 16, 16)].astype(F32)
    return norm(x.reshape(x.shape[0] * x.shape[1], x.shape[2]))


def pair_steps(plan, pair, tp, tg, bl):
    nfs = plan.nfs
    ncomp, r, cw, _ = pair.shape
    zs = [plan.copy(tp, tg.at[plan.z], plan.dp, (plan.z + k) % nfs) for k in range(1, nfs)]

    def begin():
        tg[plan.z] = tp[...]
        start(zs)

    def work(n):
        def step():
            if n == 0:
                arrive(zs)
            pw, gain = pair_params(tg)
            heads = pw.shape[0]

            def some(i, carry):
                pn, _ = pair_rows(pair, n, i)
                low = (pn * gain).astype(BF)
                parts = [dot_nt(pw, low[cw * k : cw * k + cw]) for k in range(16)]
                v = jnp.transpose(jnp.stack(parts), (1, 0, 2))
                bl[pl.ds(n * heads, heads), pl.ds(i * 16, 16), :] = v.astype(BF)
                return carry

            lax.fori_loop(0, r // 16, some, 0)

        return step

    return [begin] + [work(n) for n in range(ncomp)]


def pair_back(pair_hbm, tg, ob, pgrad, tacc):
    ncomp, r, cw, width = pair_hbm.shape
    pw, gain = pair_params(tg)
    heads = pw.shape[0]
    per = r // 16

    def run(pair, pgb, lsem, osem):
        load = pltpu.make_async_copy(pair_hbm, pair, lsem.at[0])
        load.start()
        load.wait()

        def flight(it):
            return pltpu.make_async_copy(pgb.at[it % 2], pgrad.at[it // per, pl.ds(it % per * 16, 16)], osem.at[it % 2])

        def some(it, carry):
            pwg, pgg = carry
            n, i = it // per, it % per
            pn, pr = pair_rows(pair, n, i)
            low = (pn * gain).astype(BF)
            g = jnp.transpose(ob[pl.ds(n * heads, heads), pl.ds(i * 16, 16), :], (1, 0, 2)).astype(BF)
            parts = []
            for k in range(16):
                parts.append(dot_tn(g[k], pw))
                pwg = pwg + dot(g[k], low[cw * k : cw * k + cw])
            gl = jnp.concatenate(parts, axis=0)
            pgg = pgg + jnp.sum(gl * pn, axis=0, keepdims=True)

            @pl.when(it >= 2)
            def _():
                flight(it - 2).wait()

            pgb[it % 2] = norm_back(pn, pr, gl * gain).reshape(16, cw, width)
            flight(it).start()
            return pwg, pgg

        zero = (jnp.zeros((heads, width), F32), jnp.zeros((1, width), F32))
        pwg, pgg = lax.fori_loop(0, ncomp * per, some, zero)
        for it in range(max(ncomp * per - 2, 0), ncomp * per):
            flight(it).wait()
        tacc[0, 0:16, :] = pwg
        tacc[0, 16:32, :] = jnp.broadcast_to(pgg, (16, width))

    pl.run_scoped(run, pltpu.VMEM(pair_hbm.shape, BF), pltpu.VMEM((2, 16, cw, width), F32), DMA((1,)), DMA((2,)))


def tiny_steps(plan, tacc, tr, tz, out, work):
    nfs = plan.nfs
    bs = bits_of(plan.ndp)
    cs = [plan.copy(tacc.at[i], tr.at[i], flip(plan.dp, b), plan.z) for i, b in enumerate(bs)]
    zs = [plan.copy(tacc.at[len(bs)], tz.at[k - 1], plan.dp, (plan.z + k) % nfs) for k in range(1, nfs)]

    def begin():
        work()
        cs[0].start()

    def step(i):
        def go():
            cs[i].wait_recv()
            tacc[i + 1] = tacc[i] + tr[i]
            start([cs[i + 1]] if i + 1 < len(bs) else zs)

        return go

    def total():
        arrive(zs)
        t = tacc[len(bs)]
        for k in range(nfs - 1):
            t = t + tz[k]
        out[...] = t

    return [begin] + [step(i) for i in range(len(bs))] + [total]


ANYWHERE = pl.BlockSpec(memory_space=pl.ANY)
def follow(order, lists):
    at = {k: 0 for k in lists}
    for ch in order:
        if ch in lists and at[ch] < len(lists[ch]):
            lists[ch][at[ch]]()
            at[ch] += 1
    for k, steps in lists.items():
        for step in steps[at[k] :]:
            step()


VMEM = pl.BlockSpec(memory_space=pltpu.VMEM)
SMEM = pl.BlockSpec(memory_space=pltpu.SMEM)


def fill_vectors(small, s1, rows1):
    parts = [v[...].astype(F32) for v in small]
    v = jnp.concatenate(parts[:5] + [jnp.concatenate(parts[5:], axis=1)], axis=0)
    pad = jnp.zeros((16 - v.shape[0], v.shape[1]), F32)
    s1[rows1 : rows1 + 16, 0 : v.shape[1]] = jnp.concatenate([v, pad], axis=0).astype(BF)


def forward_parts(plan, rows1, comp, cnt, x, c, g1, sm, outs, bias, wv, vs, pst, psem, fsem, during, within):
    nfs = plan.nfs
    copies = comp.shape[0]
    t, d = x.shape
    dc = c.shape[1]
    rows = t // copies
    dz, cz = d // nfs, dc // nfs
    heads = outs[-1].shape[1]
    groups = 2
    per, dg, hs = heads // groups, d // groups, d // heads
    load = plan.here(g1, wv)
    leave = [pltpu.make_async_copy(v, o, fsem.at[i]) for i, (v, o) in enumerate(zip(vs, outs))]
    fi, q, k, v, gp, sp, cl, att, gated = vs
    p = outs[-1]

    def vectors():
        parts = [jnp.zeros((16, d), F32), jnp.zeros((16, dc), F32), jnp.zeros((16, dc), F32)]
        a = lax.broadcasted_iota(jnp.int32, (dz, dc), 0)
        b = lax.broadcasted_iota(jnp.int32, (dz, dc), 1)
        for z in range(nfs):
            piece = wv[z, rows1 : rows1 + 16, :][:, :dz]
            one = jnp.where((a < cz) & (b == a + z * cz), 1.0, 0.0).astype(BF)
            two = jnp.where((a >= cz) & (b == a - cz + z * cz), 1.0, 0.0).astype(BF)
            for i, e in enumerate((place(dz, d, z * dz, True), one, two)):
                parts[i] = parts[i] + dot(piece, e)
        sm[...] = parts[0][0:8]
        sm[5:6, 0:dc] = parts[1][5:6]
        sm[6:7, 0:dc] = parts[2][5:6]

    def first():
        load.start()
        load.wait()
        vectors()

        def one(i, carry):
            at = pl.ds(pl.multiple_of(i * rows, rows), rows)

            def view(ref):
                return ref.at[at, :]

            ws = [wv.at[:, pl.ds(j * dz, dz), :] for j in range(4)]
            ws += [wv.at[:, pl.ds(4 * dz + j * cz, cz), :] for j in range(2)]
            first_kernel(view(x), view(c), *ws, sm, *[view(o) for o in vs[:7]])
            for at_i, step in during.items():
                pl.when(i == at_i)(step)
            return carry

        lax.fori_loop(0, copies, one, 0)
        start(leave[:7])

    def flight(it):
        return pltpu.make_async_copy(pst.at[it % 2], p.at[it // groups, pl.ds(it % groups * per, per)], psem.at[it % 2])

    def attend():
        def one(it, carry):
            ci, g = it // groups, it % groups
            at = pl.ds(pl.multiple_of(ci * rows, rows), rows)
            cols = pl.ds(pl.multiple_of(g * dg, dg), dg)
            n = comp[ci]

            @pl.when(it >= 2)
            def _():
                flight(it - 2).wait()

            def keep(j, val):
                pst[it % 2, j] = val

            def view(ref):
                return ref.at[at, cols]

            attend_body(per, hs, cnt[n], view(q), view(k), view(v), lambda j: bias[n * heads + g * per + j], view(gp),
                        keep, view(att), view(gated))
            flight(it).start()
            pl.when(it == copies * groups // 2)(within)
            return carry

        lax.fori_loop(0, copies * groups, one, 0)
        start(leave[7:])

    def leaving():
        for it in range(copies * groups - 2, copies * groups):
            flight(it).wait()
        for o in leave:
            o.wait()

    return first, attend, leaving


def gather_kernel(ndp, nfs, spots, rows1, with_bias, *refs):
    nw = len(spots)
    ws, small, rest = refs[:nw], refs[nw : nw + 7], refs[nw + 7 :]
    if with_bias:
        pair, tp, comp, cnt, x, c, g1, g2, tg, sm = rest[:10]
        outs, rest = rest[10:20], rest[20:]
        s1, s2, bl, zb, bias, wv, pst = rest[:7]
        vs = rest[7:16]
        send, recv, local, psem, fsem = rest[16:]
    else:
        g1, g2, s1, s2, send, recv, local = rest
    plan = Plan(ndp, nfs, send, recv, local)
    fill = {0: [], 1: []}
    for w, (which, col, width, at) in zip(ws, spots):
        src = w if width == w.shape[1] else w.at[:, pl.ds(col, width)]
        fill[which].append(plan.here(src, (s1, s2)[which].at[pl.ds(at, w.shape[0]), :]))
    start(fill[0])
    start(fill[1])
    fill_vectors(small, s1, rows1)
    plan.barrier()

    def wait(cs):
        def go():
            for c in cs:
                c.wait()

        return go

    size1 = g1.shape[1]
    half = size1 // 2
    nothing = wait([])
    if half % (16 * ndp) == 0:
        spans = [pl.ds(0, half), pl.ds(half, half)]
    else:
        spans = [pl.ds(0, size1)]
    a = [gather_steps(plan, s1.at[sp_], g1.at[:, sp_], nothing if i else wait(fill[0])) for i, sp_ in enumerate(spans)]
    c_ = gather_steps(plan, s2, g2, wait(fill[1]))
    if not with_bias:
        follow("", dict(enumerate(a + [c_])))
        plan.finish()
        return
    p = pair_steps(plan, pair, tp, tg, bl)
    ncomp = cnt.shape[0]
    heads = bl.shape[0] // ncomp
    b = []
    for n in range(ncomp):
        hs = pl.ds(n * heads, heads)
        b.append(bias_gather_steps(plan, bl.at[hs], zb.at[:, hs], bias.at[hs]))

    def both(*steps):
        def go():
            for step in steps:
                step()

        return go

    during = {0: both(b[-1][1], c_[0], b[0][2])} if ncomp > 1 else {}
    first, attend, leaving = forward_parts(
        plan, rows1, comp, cnt, x, c, g1, sm, outs, bias, wv, vs, pst, psem, fsem, during, c_[2]
    )
    run = [p[0], a[0][0], p[1], a[0][1]]
    for more in a[1:]:
        run += [more[0]]
    run += p[2:]
    for more in a[1:]:
        run += [more[1]]
    run += [b[0][0]]
    for i in range(2, len(a[0]) - 1):
        run += [more[i] for more in a]
    if ncomp > 1:
        run += [b[0][1], b[1][0]] + [b_ for more in b[1:-1] for b_ in more[1:]]
        run += [more[-1] for more in a] + [first, b[0][3], b[-1][2], c_[1], b[-1][3], b[0][4], b[-1][4]]
    else:
        run += [b[0][1], c_[0]] + [more[-1] for more in a] + [first, b[0][2], c_[1]] + b[0][3:]
    for step in run + [attend] + c_[3:] + [leaving]:
        step()
    plan.finish()


def run_gather(ndp, nfs, spots, ws, small, more, size1, size2, d, heads, rows1):
    sds = jax.ShapeDtypeStruct
    count = 80 * max(ndp // 4, 2)
    outs = [sds((nfs, size1, d), BF), sds((nfs, size2, d), BF)]
    specs = [ANYWHERE] * 2
    scratch = [pltpu.VMEM((size1, d), BF), pltpu.VMEM((size2, d), BF)]
    sems = [DMA((count,)), DMA((count,)), DMA((len(ws) + 8,))]
    ins = list(ws) + list(small)
    in_specs = [VMEM] * len(ins)
    if more is not None:
        pair, tp, comp, cnt, x, c = more
        ncomp, r, cw, _ = pair.shape
        nh, rows, full = ncomp * heads, r * ndp, cw * nfs
        t, dc = c.shape
        ins += more
        in_specs += [VMEM, VMEM, SMEM, SMEM, VMEM, VMEM]
        kept = [(t, d)] * 6 + [(t, dc)] + [(t, d)] * 2
        outs += [sds((nfs,) + tp.shape, BF), sds((8, d), F32)] + [sds(k, BF) for k in kept]
        outs += [sds((comp.shape[0], heads, rows, rows), BF)]
        specs += [VMEM, VMEM] + [ANYWHERE] * (len(kept) + 1)
        scratch += [pltpu.VMEM((nh, r, cw), BF), pltpu.VMEM((nfs, nh, r, cw), BF), pltpu.VMEM((nh, rows, full), BF),
                    pltpu.VMEM((nfs, size1, d), BF), pltpu.VMEM((2, heads // 2, rows, rows), BF)]
        scratch += [pltpu.VMEM(k, BF) for k in kept]
        sems += [DMA((2,)), DMA((len(kept),))]
    return pl.pallas_call(
        functools.partial(gather_kernel, ndp, nfs, spots, rows1, more is not None),
        in_specs=in_specs,
        out_specs=specs,
        out_shape=outs,
        scratch_shapes=scratch + sems,
        compiler_params=params(61, collective_id=0, has_side_effects=True),
        name="gather",
    )(*ins)


class Tiles:
    def __init__(self, bufs, sems):
        self.bufs, self.sems = bufs, sems
        self.held = [None] * bufs.shape[0]
        self.copies = [None] * bufs.shape[0]
        self.used = [-1] * bufs.shape[0]

    def fetch(self, key, ref, col, width, now):
        if key in self.held:
            i = self.held.index(key)
            self.used[i] = now
            return i
        i = self.used.index(min(self.used))
        self.held[i], self.used[i] = key, now
        src = ref if width == ref.shape[1] else ref.at[:, pl.ds(col, width)]
        self.copies[i] = pltpu.make_async_copy(src, self.bufs.at[i, :, pl.ds(0, width)], self.sems.at[i])
        self.copies[i].start()
        return i

    def wait(self, i):
        if self.copies[i] is not None:
            self.copies[i].wait()
            self.copies[i] = None


def attend_back_phase(comp, p, ops_hbm, outs_hbm, db, during):
    copies, heads, rows, _ = p.shape
    t, d = ops_hbm[0].shape
    ncomp = db.shape[0]
    groups = 2
    per, dg, hs = heads // groups, d // groups, d // heads
    width = min(256, dg)
    scale = hs ** (-0.5)

    def run(ops, res, pb, dbs, isem, psem, dsem, rsem):
        inds = [[jnp.full((1, rows), jnp.where(comp[c] == n, 1.0, 0.0), F32).astype(BF) for n in range(ncomp)] for c in range(copies)]
        for g in range(groups):
            cols = pl.ds(g * dg, dg)
            loads = [pltpu.make_async_copy(a.at[:, cols], ops.at[i], isem.at[i]) for i, a in enumerate(ops_hbm)]
            start(loads)

            def fetch(j, slot):
                return pltpu.make_async_copy(p.at[:, g * per + j], pb.at[slot], psem.at[slot])

            def flight(j):
                return pltpu.make_async_copy(dbs.at[j % 2], db.at[:, g * per + j], dsem.at[j % 2])

            fetch(0, 0).start()
            for c in loads:
                c.wait()
            res[...] = jnp.zeros_like(res)

            def one(j, carry):
                slot = j % 2
                fetch(j, slot).wait()

                @pl.when(j + 1 < per)
                def _():
                    fetch(j + 1, 1 - slot).start()

                @pl.when(j >= 2)
                def _():
                    flight(j - 2).wait()

                w = jnp.minimum(j * hs // 128 * 128, dg - width)
                m = lane_mask(j * hs - w, hs, width)
                win = pl.ds(pl.multiple_of(w, 128), width)
                acc = [None] * ncomp
                for c in range(copies):
                    rs = pl.ds(c * rows, rows)
                    dam = ops[3, rs, win] * m
                    delta = jnp.sum(dam.astype(F32) * ops[4, rs, win].astype(F32), axis=-1, keepdims=True)
                    pj = pb[slot, c]
                    ds = (pj.astype(F32) * (dot_nt(dam, ops[2, rs, win]) - delta)).astype(BF)
                    res[2, rs, win] += dot_tn(pj, dam).astype(BF)
                    res[0, rs, win] += (dot(ds, ops[1, rs, win] * m) * scale).astype(BF)
                    res[1, rs, win] += (dot_tn(ds, ops[0, rs, win] * m) * scale).astype(BF)
                    for n in range(ncomp):
                        term = ds * inds[c][n]
                        acc[n] = term if acc[n] is None else acc[n] + term
                for n in range(ncomp):
                    dbs[slot, n] = acc[n]
                flight(j).start()
                for jj in range(per):
                    if (g, jj) in during:
                        pl.when(j == jj)(during[(g, jj)])
                return carry

            lax.fori_loop(0, per, one, 0)
            back = [pltpu.make_async_copy(res.at[i], o.at[:, cols], rsem.at[i]) for i, o in enumerate(outs_hbm)]
            start(back)
            for c in back + [flight(per - 2), flight(per - 1)]:
                c.wait()

    pl.run_scoped(
        run, pltpu.VMEM((5, t, dg), BF), pltpu.VMEM((3, t, dg), BF), pltpu.VMEM((2, copies, rows, rows), BF),
        pltpu.VMEM((2, ncomp, rows, rows), BF), DMA((5,)), DMA((2,)), DMA((2,)), DMA((3,)),
    )


def last_phase(rows_hbm, c, gm, dcp, g1, sm, vec, outs_hbm, tb, during):
    t, d = rows_hbm[0].shape
    dc = c.shape[1]
    nfs = g1.shape[0]
    dz, cz = d // nfs, dc // nfs
    count = t // tb

    def run(wv, b6, cb, gmb, dcb, sgb, cgb, gsb, wsem, isem, osem):
        load = pltpu.make_async_copy(g1, wv, wsem.at[0])
        load.start()

        def come(i):
            at, k = pl.ds(pl.multiple_of(i * tb, tb), tb), i % 2
            pairs = [(r_.at[at, :], b6.at[k, n]) for n, r_ in enumerate(rows_hbm)]
            pairs += [(c.at[at, :], cb.at[k]), (gm.at[at, :], gmb.at[k]), (dcp.at[at, :], dcb.at[k])]
            return [pltpu.make_async_copy(a, b_, isem.at[k, n]) for n, (a, b_) in enumerate(pairs)]

        def leave(i):
            at, k = pl.ds(pl.multiple_of(i * tb, tb), tb), i % 2
            bufs = [sgb.at[k], cgb.at[k], gsb.at[k, 0], gsb.at[k, 1]]
            return [pltpu.make_async_copy(b_, o.at[at, :], osem.at[k, n]) for n, (b_, o) in enumerate(zip(bufs, outs_hbm))]

        start(come(0))
        vec[...] = jnp.zeros_like(vec)
        load.wait()
        ws = [wv.at[:, pl.ds(j * dz, dz), :] for j in range(4)]
        ws += [wv.at[:, pl.ds(4 * dz + j * cz, cz), :] for j in range(2)]

        def one(i, carry):
            k = i % 2
            for c_ in come(i):
                c_.wait()

            @pl.when(i + 1 < count)
            def _():
                start(come(i + 1))

            @pl.when(i >= 2)
            def _():
                for c_ in leave(i - 2):
                    c_.wait()

            r6 = [b6.at[k, n] for n in range(6)]
            last_body(*r6[:5], cb.at[k], r6[5], gmb.at[k], dcb.at[k], *ws, sm, sgb.at[k], cgb.at[k], gsb.at[k, 0],
                      gsb.at[k, 1], vec)
            start(leave(i))
            for ii in range(count):
                if ii in during:
                    pl.when(i == ii)(during[ii])
            return carry

        lax.fori_loop(0, count, one, 0)
        for i in range(max(count - 2, 0), count):
            for c_ in leave(i):
                c_.wait()

    pl.run_scoped(
        run, pltpu.VMEM(g1.shape, BF), pltpu.VMEM((2, 6, tb, d), BF), pltpu.VMEM((2, tb, dc), BF),
        pltpu.VMEM((2, tb, d), F32), pltpu.VMEM((2, tb, dc), F32), pltpu.VMEM((2, tb, d), F32), pltpu.VMEM((2, tb, dc), F32),
        pltpu.VMEM((2, 2, tb, d), BF), DMA((1,)), DMA((2, 9)), DMA((2, 4)),
    )


def cuts(size, unit):
    if size % (2 * unit) == 0:
        return [(0, size // 2), (size // 2, size // 2)]
    return [(0, size)]


ROWS = 384
LAST = 128
ORDERS = (
    "jjjjjSjjSjjjjT",
    {(0, 1): "T", (0, 5): "S", (1, 2): "S", (1, 6): "T"},
    {0: "b", 1: "c", 2: "T", 3: "S", 6: "b", 7: "T"},
    "ScjjjQbjQTjSjRc",
    "RSTQbRQcRtSTQRtttQRtSTQRSTQRSTQRSTQR",
)


def products_phase(jobs, ins, packs, order, step, state):
    t, d = ins[0].shape[0], packs[0].shape[2]
    nz = packs[0].shape[0]

    def run(tiles, outs, tsem, osem):
        held = Tiles(tiles, tsem)
        flying = [[] for _ in range(outs.shape[0])]
        ready = {}

        def operands(j):
            (li, lc, lw), (ri, rc, rw), _, _ = jobs[j]
            return (
                held.fetch((li, lc), ins[li], lc, lw, 2 * j),
                held.fetch((ri, rc), ins[ri], rc, rw, 2 * j + 1),
            )

        def job(j):
            if j not in ready:
                ready[j] = operands(j)
            (_, _, lw), _, which, (z0, count, (zr, at)) = jobs[j]
            li, ri = ready[j]
            held.wait(li)
            held.wait(ri)
            if j + 1 < len(jobs):
                ready[j + 1] = operands(j + 1)
            o = j % outs.shape[0]
            for c in flying[o]:
                c.wait()
            kb = min(lw, ROWS)

            def some(i, carry):
                cols = pl.ds(pl.multiple_of(i * kb, kb), kb)
                outs[o, cols, :] = dot_tn(tiles[li, :, cols], tiles[ri]).astype(BF)
                return carry

            lax.fori_loop(0, lw // kb, some, 0)
            flying[o] = [
                pltpu.make_async_copy(
                    outs.at[o, pl.ds(i * zr, zr), :], packs[which].at[z0 + i, pl.ds(at, zr), :], osem.at[o, i]
                )
                for i in range(count)
            ]
            start(flying[o])

        def settle():
            for o in range(outs.shape[0]):
                for c in flying[o]:
                    c.wait()
                flying[o] = []

        state["settle"] = settle
        j = 0
        for ch in order:
            if ch == "j":
                job(j)
                j += 1
            else:
                step(ch)
        settle()
        state["settle"] = lambda: None

    pl.run_scoped(run, pltpu.VMEM((4, t, d), BF), pltpu.VMEM((2, d, d), BF), DMA((4,)), DMA((2, nz)))


def products_kernel(ndp, nfs, jobs, split, orders, nin, small_at, cuts1, cuts2, full, *refs):
    ins, rest = list(refs[:nin]), list(refs[nin:])

    def take(n):
        out = rest[:n]
        del rest[:n]
        return out

    if full:
        p, q, k, v, da, att, x, c, sp, gm, dcp, g1, sm, vec_a, comp, pair, tg = take(17)
    else:
        (small,) = take(1)
    r1, r2, pg1, pg2 = take(4)
    if full:
        dq, dk, dv, gsc, gsh, db, sg, cg, pgrad, tiny_out = take(10)
    per = 5
    bufs1 = [take(per) for _ in cuts1]
    bufs2 = [take(per) for _ in cuts2]
    send, recv, local = take(3)
    if full:
        small, vec = take(2)
        ins += [dq, dk, dv, gsc, gsh]
    plan = Plan(ndp, nfs, send, recv, local)
    state = {"settle": lambda: None}
    lsmall = plan.here(small, pg1.at[:, pl.ds(small_at, 16), :])

    def settle():
        state["settle"]()

    def settle_small():
        settle()
        if full:
            both = jnp.concatenate([vec_a[...] + vec[...], jnp.zeros_like(vec)], axis=0).astype(BF)
            d, dc = x.shape[1], c.shape[1]
            dz, cz = d // nfs, dc // nfs
            row = lax.broadcasted_iota(jnp.int32, (16, 1), 0)
            small[...] = jnp.zeros_like(small)
            for z in range(nfs):
                wide = dot(both, place(dz, d, z * dz, False))
                thin = dot(both[:, :dc], place(dz, dc, z * cz, False))
                small[z, :, 0:dz] = jnp.where((row == 5) | (row == 6), thin, wide).astype(BF)
        lsmall.start()
        lsmall.wait()

    def chunks(pg, out, bufs, spans, last):
        done = []
        for i, (buf, span) in enumerate(zip(bufs, spans)):
            at = pl.ds(*span)
            done.append(reduce_steps(plan, pg.at[:, at], out.at[at], *buf, last if i == len(bufs) - 1 else settle))
        return done

    lists = {"STU"[i]: steps for i, steps in enumerate(chunks(pg2, r2, bufs2, cuts2, settle))}
    lists.update({"QR"[i]: steps for i, steps in enumerate(chunks(pg1, r1, bufs1, cuts1, settle_small))})
    if full:
        (ob,) = take(1)
        ncomp = db.shape[0]
        heads = ob.shape[0] // ncomp
        for n in range(ncomp):
            lists["bc"[n]] = bias_reduce_steps(plan, db.at[n], ob.at[pl.ds(n * heads, heads)], *take(5))
        tacc, tr, tz = take(3)
        lists["t"] = tiny_steps(plan, tacc, tr, tz, tiny_out, lambda: pair_back(pair, tg, ob, pgrad, tacc))
    left = {name: list(steps) for name, steps in lists.items()}

    def step(ch):
        if left.get(ch):
            left[ch].pop(0)()

    def steps_of(table):
        return {key: (lambda chs: lambda: [step(ch) for ch in chs] and None)(chs) for key, chs in table.items()}

    first, in_attend, in_last, second, tail = orders
    plan.barrier()
    products_phase(jobs[:split], ins, (pg1, pg2), first, step, state)
    if full:
        attend_back_phase(comp, p, (q, k, v, da, att), (dq, dk, dv), db, steps_of(in_attend))
        step("b")
        step("c")
        last_phase((dq, dk, dv, ins[14], x, sp), c, gm, dcp, g1, sm, vec, (sg, cg, gsc, gsh), LAST, steps_of(in_last))
    products_phase(jobs[split:], ins, (pg1, pg2), second, step, state)
    for ch in tail:
        step(ch)
    for name in left:
        while left[name]:
            step(name)
    plan.finish()


def run_products(ndp, nfs, jobs, split, orders, ins, more, small, small_at, size1, size2):
    t = ins[0].shape[0]
    d = ins[1].shape[1]
    nchip = ndp // 2
    sds = jax.ShapeDtypeStruct

    def sums(*shape):
        return [pltpu.VMEM((nchip,) + shape, BF), pltpu.VMEM((nchip,) + shape, BF), pltpu.VMEM((max(nchip - 1, 1),) + shape, BF)]

    cuts1, cuts2 = cuts(size1, 16 * ndp), cuts(size2, 16 * ndp)

    def scratch(spans):
        got = []
        for _, size in spans:
            n = size // ndp
            got += sums(nfs, n, d) + [pltpu.VMEM((nfs - 1, n, d), BF), pltpu.VMEM((n, d), BF)]
        return got

    count = 100 * max(ndp // 4, 2)
    outs = [sds((size1, d), BF), sds((size2, d), BF), sds((nfs, size1, d), BF), sds((nfs, size2, d), BF)]
    out_specs = [ANYWHERE] * 4
    in_specs = [ANYWHERE] * len(ins)
    tail_scratch = []
    if more is not None:
        p, pair, dc = more[0], more[15], more[7].shape[1]
        _, heads, rows, full = p.shape
        ncomp, r, cw, width = pair.shape
        levels = len(bits_of(ndp))
        in_specs += [ANYWHERE] * 12 + [VMEM, VMEM, SMEM, ANYWHERE, VMEM]
        extra = list(more)
        outs += [sds((t, d), BF)] * 5 + [sds((ncomp, heads, rows, full), BF), sds((t, d), F32), sds((t, dc), F32),
                                         sds(pair.shape, F32), sds((32, width), F32)]
        out_specs += [ANYWHERE] * 9 + [VMEM]
        tail_scratch = [pltpu.VMEM((nfs, 16, d), BF), pltpu.VMEM((8, d), F32), pltpu.VMEM((ncomp * heads, r, cw), F32)]
        tail_scratch += (sums(heads, r, full) + [pltpu.VMEM((nfs, heads, r, cw), BF), pltpu.VMEM((nfs - 1, heads, r, cw), BF)]) * ncomp
        tail_scratch += [pltpu.VMEM((k, 32, width), F32) for k in (levels + 1, levels, nfs - 1)]
    else:
        in_specs += [VMEM]
        extra = [small]
    return pl.pallas_call(
        functools.partial(products_kernel, ndp, nfs, jobs, split, orders, len(ins), small_at, cuts1, cuts2,
                          more is not None),
        in_specs=in_specs,
        out_specs=out_specs,
        out_shape=outs,
        scratch_shapes=scratch(cuts1) + scratch(cuts2)
        + [DMA((count,)), DMA((count,)), DMA((8 * nchip + 10,))] + tail_scratch,
        compiler_params=params(62, collective_id=1, has_side_effects=True),
        name="products",
    )(*ins, *extra)


def emit_kernel(spots, r1, r2, *outs):
    for o, (which, at) in zip(outs, spots):
        r = (r1, r2)[which]
        n = o.shape[0]
        for i, row in enumerate(at):
            w = r.shape[1]
            o[:, i * w : i * w + w] = r[row : row + n, :].astype(F32)


def run_emit(r1, r2, spots, shapes):
    sds = jax.ShapeDtypeStruct
    return pl.pallas_call(
        functools.partial(emit_kernel, spots),
        in_specs=[VMEM] * 2,
        out_specs=[VMEM] * len(shapes),
        out_shape=[sds(k, F32) for k in shapes],
        compiler_params=params(40),
        name="emit",
    )(r1, r2)


def body(ndp, nfs, *args):
    (single, condition, pair_tensor, counts, complex_of, cotangent, condition_gain, scale_weight, scale_bias,
     shift_weight, query_weight, query_bias, key_weight, value_weight, gate_weight, output_weight, pair_gain,
     pair_weight, branch_gate_weight, branch_gate_bias, transition_gain, transition_scale_weight,
     transition_scale_bias, transition_shift_weight, hidden_gate, hidden_value, hidden_output, final_gate_weight,
     final_gate_bias) = args
    copies, rows, d = single.shape
    dc = condition.shape[2]
    t = copies * rows
    heads = pair_weight.shape[1]
    ncomp = counts.shape[0]
    dz = d // nfs
    x = single.reshape(t, d)
    c = condition.reshape(t, dc)
    ct = cotangent.reshape(t, d)
    unit = 16 * ndp

    def padded(total):
        return -(-total // unit) * unit

    vectors = (scale_bias, query_bias, branch_gate_bias, transition_scale_bias, final_gate_bias,
               condition_gain, transition_gain)
    small = [v[None, :] for v in vectors]
    cz, fz = dc // nfs, hidden_output.shape[0]
    rows1 = 4 * dz + 2 * cz
    rows2 = fz + 5 * dz + 4 * cz
    size1, size2 = padded(rows1 + 16), padded(rows2)
    ws, spots = [], []

    def spot(w, which, at, col=0):
        ws.append(w)
        spots.append((which, col, d, at))

    for i, w in enumerate((query_weight, key_weight, value_weight, gate_weight)):
        spot(w, 0, i * dz)
    spot(scale_weight, 0, 4 * dz)
    spot(shift_weight, 0, 4 * dz + cz)
    spot(hidden_output, 1, 0)
    spot(output_weight, 1, fz)
    for i, (w, col) in enumerate(((hidden_gate, 0), (hidden_gate, d), (hidden_value, 0), (hidden_value, d))):
        spot(w, 1, fz + (i + 1) * dz, col)
    for i, w in enumerate((branch_gate_weight, transition_scale_weight, transition_shift_weight, final_gate_weight)):
        spot(w, 1, fz + 5 * dz + i * cz)
    pair_width = pair_weight.shape[0] * nfs
    local_rows, local_cols = pair_tensor.shape[1:3]
    pgw = jnp.concatenate([pair_weight, pair_gain[:, None]], axis=1)
    aligned = local_rows % 16 == 0 and heads == 16 and pair_width == 128
    if aligned:
        tp = jnp.pad(pgw, ((0, 0), (0, pair_width - heads - 1)))
        more = [pair_tensor, tp, complex_of, counts, x, c]
        g1, g2, tg, sm, first_in, q, k, v, gp, sp, cl1, att, gated, p = run_gather(
            ndp, nfs, tuple(spots), ws, small, more, size1, size2, d, heads, rows1
        )
    else:
        pgw = lax.all_gather(pgw, FS, axis=0, tiled=True)
        pw, pgain = pgw[:, :heads], pgw[:, heads].astype(F32)
        pair_norm, pair_rstd = norm(pair_tensor.astype(F32))
        pair_low = (pair_norm * pgain).astype(BF)
        bias_local = jnp.transpose(dot(pair_low, pw).astype(BF), (0, 3, 1, 2))
        g1, g2 = run_gather(ndp, nfs, tuple(spots), ws, small, None, size1, size2, d, heads, rows1)
        bias = lax.all_gather(bias_local, FS, axis=3, tiled=True)
        bias = lax.all_gather(bias, DP, axis=2, tiled=True)
        tg = None
        sm = jnp.transpose(g1[:, rows1 : rows1 + 8, :dz], (1, 0, 2)).reshape(8, d).astype(F32)
        gains = g1[:, rows1 + 5, : 2 * cz].reshape(nfs, 2, cz)
        gains = jnp.transpose(gains, (1, 0, 2)).reshape(2, dc).astype(F32)
        sm = jnp.concatenate([sm[:5], jnp.pad(gains, ((0, 0), (0, d - dc))), sm[7:]], axis=0)
        first_in, q, k, v, gp, sp, cl1 = run_first(x, c, g1, sm, rows)
        p, att, gated = run_attend(complex_of, counts, q, k, v, gp, bias, 2)

    (out, gm, dcp, si, act, cl2, gt2, gz2, gh, gv, gsc2, gsh2, gt1, gz1, da, dg, vec_a) = run_middle(
        complex_of, counts, x, c, ct, gated, att, gp, g2, sm, rows
    )
    small_grad = None
    if not aligned:
        dq, dk, dv, db = run_attend_back(complex_of, p, q, k, v, da, att, ncomp, 2)
        sgrad, cgrad, gsc1, gsh1, vec_b = run_last(dq, dk, dv, dg, x, c, sp, gm, dcp, g1, sm, rows)
        vec = (vec_a + vec_b).astype(BF)
        vz = jnp.transpose(vec.reshape(8, nfs, dz), (1, 0, 2))
        cv = jnp.transpose(vec[5:7, :dc].reshape(2, nfs, cz), (1, 0, 2))
        vz = jnp.concatenate(
            [vz[:, :5], jnp.pad(cv, ((0, 0), (0, 0), (0, dz - cz))), jnp.zeros((nfs, 9, dz), BF)], axis=1
        )
        small_grad = jnp.pad(vz, ((0, 0), (0, 0), (0, d - dz)))
    ins = [act, gt2, si, gh, gv, gated, gt1, c, gz1, gz2, cl2, gsc2, gsh2, first_in, dg, cl1]
    hz = nfs // 2

    def job(li, lc, lw, ri, rc, which, at):
        if lw == dc:
            where = (0, nfs, (cz, at))
        elif li == 0:
            where = (lc // d * hz, hz, (fz, at))
        else:
            where = (0, nfs, (dz, at))
        return ((li, lc, lw), (ri, rc, d), which, where)

    c0 = fz + 5 * dz
    jobs = [
        job(0, 0, d, 1, 0, 1, 0), job(0, d, d, 1, 0, 1, 0),
        job(2, 0, d, 3, 0, 1, fz + dz), job(2, 0, d, 3, d, 1, fz + 2 * dz),
        job(5, 0, d, 6, 0, 1, fz),
        job(2, 0, d, 4, 0, 1, fz + 3 * dz), job(2, 0, d, 4, d, 1, fz + 4 * dz),
        job(7, 0, dc, 8, 0, 1, c0), job(7, 0, dc, 9, 0, 1, c0 + 3 * cz),
        job(10, 0, dc, 11, 0, 1, c0 + cz), job(10, 0, dc, 12, 0, 1, c0 + 2 * cz),
        job(13, 0, d, 16, 0, 0, 0), job(13, 0, d, 17, 0, 0, dz), job(13, 0, d, 18, 0, 0, 2 * dz),
        job(13, 0, d, 14, 0, 0, 3 * dz),
        job(15, 0, dc, 19, 0, 0, 4 * dz), job(15, 0, dc, 20, 0, 0, 4 * dz + cz),
    ]
    if aligned:
        more = [p, q, k, v, da, att, x, c, sp, gm, dcp, g1, sm, vec_a, complex_of, pair_tensor, tg]
    else:
        more = None
        ins += [dq, dk, dv, gsc1, gsh1]
    moved = run_products(ndp, nfs, jobs, 11, ORDERS, ins, more, small_grad, rows1, size1, size2)
    r1, r2 = moved[:2]
    pz = pair_width // nfs
    if aligned:
        sgrad, cgrad, pair_grad = moved[10:13]
        tiny = lax.dynamic_slice_in_dim(moved[13][: heads + 1], lax.axis_index(FS) * pz, pz, axis=1).T
    else:
        bias_sum = lax.psum_scatter(db, DP, scatter_dimension=2, tiled=True)
        bias_sum = lax.psum_scatter(bias_sum, FS, scatter_dimension=3, tiled=True)
        bias_grad = jnp.transpose(bias_sum, (0, 2, 3, 1))
        pw_grad = dot_tn(pair_low.reshape(-1, pair_width), bias_grad.reshape(-1, heads))
        grad_low = dot(bias_grad, pw.T)
        pgain_grad = jnp.sum(grad_low * pair_norm, axis=(0, 1, 2))
        pair_grad = norm_back(pair_norm, pair_rstd, grad_low * pgain)
        tiny = lax.psum(jnp.concatenate([pw_grad, pgain_grad[:, None]], axis=1), (DP, FS))
        tiny = lax.dynamic_slice_in_dim(tiny, lax.axis_index(FS) * pz, pz, axis=0)
    sv = r1[rows1 : rows1 + 8].astype(F32)
    at = fz + 5 * dz
    spots = tuple((0, (i * dz,)) for i in range(4)) + tuple((0, (4 * dz + i * cz,)) for i in range(2))
    spots += ((1, (fz,)), (1, (fz + dz, fz + 2 * dz)), (1, (fz + 3 * dz, fz + 4 * dz)), (1, (0,)))
    spots += tuple((1, (at + i * cz,)) for i in range(4))
    shapes = [(dz, d)] * 4 + [(cz, d)] * 2 + [(dz, d), (dz, 2 * d), (dz, 2 * d), (fz, d)] + [(cz, d)] * 4
    w = run_emit(r1, r2, spots, shapes)
    o1, s1, o2, c2 = w[:4], w[4:6], w[6:10], w[10:]
    shape3 = (copies, rows, d)
    return (
        out.reshape(shape3),
        sgrad.reshape(shape3),
        cgrad.reshape(copies, rows, dc),
        pair_grad,
        sv[5, :cz],
        s1[0],
        sv[0, :dz],
        s1[1],
        o1[0],
        sv[1, :dz],
        o1[1],
        o1[2],
        o1[3],
        o2[0],
        tiny[:, heads],
        tiny[:, :heads],
        c2[0],
        sv[2, :dz],
        sv[6, :cz],
        c2[1],
        sv[3, :dz],
        c2[2],
        o2[1],
        o2[2],
        o2[3],
        c2[3],
        sv[4, :dz],
    )


def solution(mesh):
    both = (DP, FS)
    wide = P(both, None, None)
    mat = P(FS, None)
    vec = P(FS)
    pair = P(None, DP, FS, None)
    weights = (vec, mat, vec, mat, mat, vec, mat, mat, mat, mat, vec, mat, mat, vec, vec, mat, vec, mat, mat, mat,
               mat, mat, vec)
    in_specs = (wide, wide, pair, P(), P(both), wide) + weights
    out_specs = (wide, wide, wide, pair) + weights
    run = functools.partial(body, mesh.shape[DP], mesh.shape[FS])
    return jax.shard_map(run, mesh=mesh, in_specs=in_specs, out_specs=out_specs, check_vma=False)
```

```python
import functools

import jax
import jax.numpy as jnp
from jax import lax
from jax.experimental import pallas as pl
from jax.experimental.pallas import tpu as pltpu
from jax.sharding import PartitionSpec as P

BF = jnp.bfloat16
F32 = jnp.float32
EPSILON = 1e-05
DP = "dp"
FS = "fsdp"
MIB = 1024 * 1024
NEGATIVE = -1000000000.0


def norm(v):
    c = v - jnp.mean(v, axis=-1, keepdims=True)
    r = lax.rsqrt(jnp.mean(c * c, axis=-1, keepdims=True) + EPSILON)
    return c * r, r


def norm_back(n, r, u):
    return r * (u - jnp.mean(u, axis=-1, keepdims=True) - n * jnp.mean(u * n, axis=-1, keepdims=True))


def sig(v):
    return 0.5 * jnp.tanh(0.5 * v) + 0.5


def dot(a, b):
    return jnp.dot(a, b, preferred_element_type=F32)


def dot_nt(a, b):
    return lax.dot_general(a, b, (((1,), (1,)), ((), ())), preferred_element_type=F32)


def dot_tn(a, b):
    return lax.dot_general(a, b, (((0,), (0,)), ((), ())), preferred_element_type=F32)


def flat(ref):
    v = ref[...]
    return v.reshape(v.shape[0] * v.shape[1], v.shape[2])


def colsum(v):
    return jnp.sum(v.astype(F32), axis=0, keepdims=True)


def first_kernel(x, c, wq, wk, wv, wg, ws, wh, sm, fi, q, k, v, gp, sp, cl):
    cn, _ = norm(c[...].astype(F32))
    low = (cn * sm[5:6, : cn.shape[1]]).astype(BF)
    cl[...] = low
    pre = dot(low, flat(ws)) + sm[0:1, :]
    shift = dot(low, flat(wh))
    sp[...] = pre.astype(BF)
    an, _ = norm(x[...].astype(F32))
    first = (sig(pre) * an + shift).astype(BF)
    fi[...] = first
    q[...] = (dot(first, flat(wq)) + sm[1:2, :]).astype(BF)
    k[...] = dot(first, flat(wk)).astype(BF)
    v[...] = dot(first, flat(wv)).astype(BF)
    gp[...] = dot(first, flat(wg)).astype(BF)


def whole(shape):
    return pl.BlockSpec(shape, lambda *i: (0,) * len(shape), pipeline_mode=pl.Buffered(1))


def part(z, rows, width, at):
    return pl.BlockSpec((z, rows, width), lambda *i: (0, at, 0), pipeline_mode=pl.Buffered(1))


def rows_of(tb, width):
    return pl.BlockSpec((tb, width), lambda i, *_: (i, 0))


def params(limit, **kw):
    return pltpu.CompilerParams(vmem_limit_bytes=limit * MIB, **kw)


def cost(flops, nbytes, trans=0):
    return pl.CostEstimate(flops=int(flops), bytes_accessed=int(nbytes), transcendentals=int(trans))


def run_first(x, c, g1, sm, tb):
    t, d = x.shape
    dc = c.shape[1]
    z = g1.shape[0]
    dz, cz = d // z, dc // z
    sds = jax.ShapeDtypeStruct
    return pl.pallas_call(
        first_kernel,
        grid=(t // tb,),
        in_specs=[rows_of(tb, d), rows_of(tb, dc)]
        + [part(z, dz, d, i) for i in range(4)]
        + [part(z, cz, d, 4 * dz // cz), part(z, cz, d, 4 * dz // cz + 1), whole(sm.shape)],
        out_specs=[rows_of(tb, d)] * 6 + [rows_of(tb, dc)],
        out_shape=[sds((t, d), BF)] * 6 + [sds((t, dc), BF)],
        compiler_params=params(60),
        cost_estimate=cost(2 * t * d * (4 * d + 2 * dc), 20 * MIB),
        name="first",
    )(x, c, g1, g1, g1, g1, g1, g1, sm)


def windows(per, hs):
    out = []
    for j in range(per):
        lo = j * hs
        w = min(lo // 128 * 128, max(per * hs - 256, 0))
        out.append((w, lo - w))
    return out


def lane_mask(o, hs, width):
    lane = lax.broadcasted_iota(jnp.int32, (1, width), 1)
    return jnp.where((lane >= o) & (lane < o + hs), 1.0, 0.0).astype(BF)


def put(acc, w, width, val):
    for b in range(width // 128):
        key = w // 128 + b
        piece = val[:, 128 * b : 128 * b + 128]
        acc[key] = piece if key not in acc else acc[key] + piece


def attend_body(per, hs, limit, q, k, v, bias_of, gp, keep, att, gated):
    width = min(256, per * hs)
    mrow = jnp.where(
        lax.broadcasted_iota(jnp.int32, (1, k.shape[0]), 1) < limit, 0.0, NEGATIVE
    ).astype(F32)
    scale = hs ** (-0.5)
    acc = {}
    for j, (w, o) in enumerate(windows(per, hs)):
        m = lane_mask(o, hs, width)
        s = dot_nt(q[:, w : w + width] * m, k[:, w : w + width]) * scale
        s = s + (bias_of(j).astype(F32) + mrow)
        e = jnp.exp(s - jnp.max(s, axis=-1, keepdims=True))
        pb = (e * (1.0 / jnp.sum(e, axis=-1, keepdims=True))).astype(BF)
        keep(j, pb)
        put(acc, w, width, dot(pb, v[:, w : w + width] * m))
    for key, val in acc.items():
        cols = slice(128 * key, 128 * key + 128)
        att[:, cols] = val.astype(BF)
        gated[:, cols] = (sig(gp[:, cols].astype(F32)) * val).astype(BF)


def attend_kernel(per, hs, comp, cnt, q, k, v, b, gp, p_out, att, gated):
    def keep(j, val):
        p_out[0, j] = val

    limit = cnt[comp[pl.program_id(0)]]
    attend_body(per, hs, limit, q, k, v, lambda j: b[0, j], gp, keep, att, gated)


def run_attend(comp, cnt, q, k, v, gp, bias, groups):
    copies = comp.shape[0]
    t, d = q.shape
    rows = t // copies
    heads = bias.shape[1]
    per, dg = heads // groups, d // groups
    blk = pl.BlockSpec((rows, dg), lambda c, g, *_: (c, g))
    sds = jax.ShapeDtypeStruct
    return pl.pallas_call(
        functools.partial(attend_kernel, per, d // heads),
        grid_spec=pltpu.PrefetchScalarGridSpec(
            num_scalar_prefetch=2,
            grid=(copies, groups),
            in_specs=[
                blk,
                blk,
                blk,
                pl.BlockSpec((1, per, rows, rows), lambda c, g, comp, cnt: (comp[c], g, 0, 0)),
                blk,
            ],
            out_specs=[
                pl.BlockSpec((1, per, rows, rows), lambda c, g, *_: (c, g, 0, 0)),
                blk,
                blk,
            ],
        ),
        out_shape=[sds((copies, heads, rows, rows), BF), sds((t, d), BF), sds((t, d), BF)],
        compiler_params=params(60),
        cost_estimate=cost(2 * 2 * t * rows * heads * 256, 40 * MIB, t * rows * heads),
        name="attend",
    )(comp, cnt, q, k, v, bias, gp)


def attend_back_kernel(per, hs, comp, p, q, k, v, da, at, dq, dk, dv, db, acc):
    c = pl.program_id(1)
    last = pl.num_programs(1) - 1
    n = comp[c]
    width = min(256, per * hs)
    scale = hs ** (-0.5)

    @pl.when(c == 0)
    def _():
        acc[...] = jnp.zeros_like(acc)

    aq, ak, av = {}, {}, {}
    prod = da[...].astype(F32) * at[...].astype(F32)
    lane = lax.broadcasted_iota(jnp.int32, (1, per * hs), 1)
    for j, (w, o) in enumerate(windows(per, hs)):
        m = lane_mask(o, hs, width)
        lo = w + o
        inside = (lane >= lo) & (lane < lo + hs)
        delta = jnp.sum(jnp.where(inside, prod, 0.0), axis=-1, keepdims=True)
        pj = p[0, j]
        win = slice(w, w + width)
        dam = da[:, win] * m
        dp = dot_nt(dam, v[:, win])
        ds = pj.astype(F32) * (dp - delta)
        acc[n, j] += ds
        dsb = ds.astype(BF)
        put(av, w, width, dot_tn(pj, dam))
        put(aq, w, width, dot(dsb, k[:, win] * m))
        put(ak, w, width, dot_tn(dsb, q[:, win] * m))
    for key in aq:
        cols = slice(128 * key, 128 * key + 128)
        dq[:, cols] = (aq[key] * scale).astype(BF)
        dk[:, cols] = (ak[key] * scale).astype(BF)
        dv[:, cols] = av[key].astype(BF)

    @pl.when(c == last)
    def _():
        db[...] = acc[...].astype(BF)


def run_attend_back(comp, p, q, k, v, da, att, ncomp, groups):
    copies, heads, rows, _ = p.shape
    t, d = q.shape
    per, dg = heads // groups, d // groups
    blk = pl.BlockSpec((rows, dg), lambda g, c, *_: (c, g))
    sds = jax.ShapeDtypeStruct
    return pl.pallas_call(
        functools.partial(attend_back_kernel, per, d // heads),
        grid_spec=pltpu.PrefetchScalarGridSpec(
            num_scalar_prefetch=1,
            grid=(groups, copies),
            in_specs=[pl.BlockSpec((1, per, rows, rows), lambda g, c, *_: (c, g, 0, 0))]
            + [blk] * 5,
            out_specs=[blk] * 3
            + [
                pl.BlockSpec(
                    (ncomp, per, rows, rows),
                    lambda g, c, *_: (0, g, 0, 0),
                    pipeline_mode=pl.Buffered(1),
                )
            ],
            scratch_shapes=[pltpu.VMEM((ncomp, per, rows, rows), F32)],
        ),
        out_shape=[sds((t, d), BF)] * 3 + [sds((ncomp, heads, rows, rows), BF)],
        compiler_params=params(60),
        cost_estimate=cost(4 * 2 * t * rows * heads * 256, 40 * MIB),
        name="attend_back",
    )(comp, p, q, k, v, da, att)


def middle_kernel(per_copy, comp, cnt, x, c, ct, gat, att, gp, wo, hl, hr, vl, vr, ho, bg, ts, th, fg, sm,
                  out, gm_o, dc_o, si_o, act_o, cl_o, g2_o, gz2_o, gh_o, gv_o, gsc_o, gsh_o, g1_o, gz1_o, da_o, dg_o, vec):
    i = pl.program_id(0)
    tb, d = x.shape
    dc = c.shape[1]
    copy = i // per_copy
    limit = cnt[comp[copy]] - (i % per_copy) * tb
    keep = jnp.where(lax.broadcasted_iota(jnp.int32, (tb, 1), 0) < limit, 1.0, 0.0).astype(F32)

    low = c[...]
    y1 = dot(gat[...], flat(wo))
    z1 = sig(dot(low, flat(bg)) + sm[2:3, :])
    kz1 = keep * z1
    mid = x[...].astype(F32) + kz1 * y1
    cn, cr = norm(low.astype(F32))
    gain = sm[6:7, :dc]
    cl = (cn * gain).astype(BF)
    cl_o[...] = cl
    s2 = sig(dot(cl, flat(ts)) + sm[3:4, :])
    mn, mr = norm(mid)
    si = (s2 * mn + dot(cl, flat(th))).astype(BF)
    si_o[...] = si
    zh = ho.shape[0] // 2
    kept = []
    y2 = None
    for half, (hg, hv) in enumerate(((hl, vl), (hr, vr))):
        u = dot(si, flat(hg))
        w = dot(si, flat(hv))
        su = sig(u)
        silu = u * su
        act = (silu * w).astype(BF)
        act_o[:, half * d : half * d + d] = act
        kept.append((w * su * (1.0 + u - silu), silu))
        hov = ho[half * zh : half * zh + zh]
        term = dot(act, hov.reshape(d, d))
        y2 = term if y2 is None else y2 + term
    z2 = sig(dot(low, flat(fg)) + sm[4:5, :])
    g = ct[...].astype(F32)
    kz2 = keep * z2
    out[...] = (mid + kz2 * y2).astype(BF)
    gk = g * kz2
    g2 = gk.astype(BF)
    gz2 = (gk * y2 * (1.0 - z2)).astype(BF)
    g2_o[...] = g2
    gz2_o[...] = gz2
    e = None
    for half, (hg, hv) in enumerate(((hl, vl), (hr, vr))):
        hov = ho[half * zh : half * zh + zh]
        ga = dot_nt(g2, hov.reshape(d, d))
        du, silu = kept[half]
        gh = (ga * du).astype(BF)
        gv = (ga * silu).astype(BF)
        gh_o[:, half * d : half * d + d] = gh
        gv_o[:, half * d : half * d + d] = gv
        term = dot_nt(gh, flat(hg)) + dot_nt(gv, flat(hv))
        e = term if e is None else e + term
    t = e * s2
    gsc = (t * mn * (1.0 - s2)).astype(BF)
    gsh = e.astype(BF)
    gsc_o[...] = gsc
    gsh_o[...] = gsh
    gc = dot_nt(gsc, flat(ts)) + dot_nt(gsh, flat(th))
    gm = g + norm_back(mn, mr, t)
    gm_o[...] = gm
    kz = gm * kz1
    g1 = kz.astype(BF)
    gz1 = (kz * y1 * (1.0 - z1)).astype(BF)
    g1_o[...] = g1
    gz1_o[...] = gz1
    dc_o[...] = norm_back(cn, cr, gc * gain) + dot_nt(gz2, flat(fg)) + dot_nt(gz1, flat(bg))
    gg = dot_nt(g1, flat(wo))
    sp = sig(gp[...].astype(F32))
    da = gg * sp
    da_o[...] = da.astype(BF)
    dg_o[...] = (da * att[...].astype(F32) * (1.0 - sp)).astype(BF)

    @pl.when(i == 0)
    def _():
        vec[...] = jnp.zeros_like(vec)

    vec[2:3, :] += colsum(gz1)
    vec[3:4, :] += colsum(gsc)
    vec[4:5, :] += colsum(gz2)
    vec[6:7, :dc] += jnp.sum(gc * cn, axis=0, keepdims=True)


def run_middle(comp, cnt, x, c, ct, gat, att, gp, g2, sm, tb):
    t, d = x.shape
    dc = c.shape[1]
    z = g2.shape[0]
    ff = 2 * d
    dz, cz, fz = d // z, dc // z, ff // z
    sds = jax.ShapeDtypeStruct
    per_copy = t // comp.shape[0] // tb
    w9 = (fz + 5 * dz) // cz
    outs = [
        (d, BF), (d, F32), (dc, F32), (d, BF), (ff, BF), (dc, BF), (d, BF), (d, BF), (ff, BF), (ff, BF),
        (d, BF), (d, BF), (d, BF), (d, BF), (d, BF), (d, BF),
    ]
    return pl.pallas_call(
        functools.partial(middle_kernel, per_copy),
        grid_spec=pltpu.PrefetchScalarGridSpec(
            num_scalar_prefetch=2,
            grid=(t // tb,),
            in_specs=[rows_of(tb, d), rows_of(tb, dc)]
            + [rows_of(tb, d)] * 4
            + [part(z, dz, d, fz // dz + i) for i in range(5)]
            + [part(z, fz, d, 0)]
            + [part(z, cz, d, w9 + i) for i in range(4)]
            + [whole(sm.shape)],
            out_specs=[rows_of(tb, w) for w, _ in outs] + [whole((8, d))],
        ),
        out_shape=[sds((t, w), k) for w, k in outs] + [sds((8, d), F32)],
        compiler_params=params(60),
        cost_estimate=cost(2 * t * (2 * d * d + 8 * d * dc + 6 * d * ff), 60 * MIB),
        name="middle",
    )(comp, cnt, x, c, ct, gat, att, gp, g2, g2, g2, g2, g2, g2, g2, g2, g2, g2, sm)


def last_body(dq, dk, dv, dg, x, c, sp, gm, dcp, wq, wk, wv, wg, ws, wh, sm, sg_o, cg_o, gsc_o, gsh_o, vec):
    dc = c.shape[1]
    e = (
        dot_nt(dq[...], flat(wq))
        + dot_nt(dk[...], flat(wk))
        + dot_nt(dv[...], flat(wv))
        + dot_nt(dg[...], flat(wg))
    )
    an, ar = norm(x[...].astype(F32))
    s = sig(sp[...].astype(F32))
    t = e * s
    gsc = (t * an * (1.0 - s)).astype(BF)
    gsh = e.astype(BF)
    gsc_o[...] = gsc
    gsh_o[...] = gsh
    sg_o[...] = gm[...] + norm_back(an, ar, t)
    gc = dot_nt(gsc, flat(ws)) + dot_nt(gsh, flat(wh))
    cn, cr = norm(c[...].astype(F32))
    cg_o[...] = dcp[...] + norm_back(cn, cr, gc * sm[5:6, :dc])
    vec[0:1, :] += colsum(gsc)
    vec[1:2, :] += colsum(dq[...])
    vec[5:6, :dc] += jnp.sum(gc * cn, axis=0, keepdims=True)


def last_kernel(*refs):
    @pl.when(pl.program_id(0) == 0)
    def _():
        refs[-1][...] = jnp.zeros_like(refs[-1])

    last_body(*refs)


def run_last(dq, dk, dv, dg, x, c, sp, gm, dcp, g1, sm, tb):
    t, d = x.shape
    dc = c.shape[1]
    z = g1.shape[0]
    dz, cz = d // z, dc // z
    sds = jax.ShapeDtypeStruct
    return pl.pallas_call(
        last_kernel,
        grid=(t // tb,),
        in_specs=[rows_of(tb, d)] * 5
        + [rows_of(tb, dc), rows_of(tb, d), rows_of(tb, d), rows_of(tb, dc)]
        + [part(z, dz, d, i) for i in range(4)]
        + [part(z, cz, d, 4 * dz // cz), part(z, cz, d, 4 * dz // cz + 1), whole(sm.shape)],
        out_specs=[rows_of(tb, d), rows_of(tb, dc), rows_of(tb, d), rows_of(tb, d), whole((8, d))],
        out_shape=[sds((t, d), F32), sds((t, dc), F32), sds((t, d), BF), sds((t, d), BF), sds((8, d), F32)],
        compiler_params=params(60),
        cost_estimate=cost(2 * t * d * (4 * d + 2 * dc), 30 * MIB),
        name="last",
    )(dq, dk, dv, dg, x, c, sp, gm, dcp, g1, g1, g1, g1, g1, g1, sm)


def flip(i, b):
    return i + b * (1 - 2 * ((i // b) % 2))


def flips(i, bs):
    for b in bs:
        i = flip(i, b)
    return i


def subsets(bs):
    out = [()]
    for b in bs:
        out = out + [s + (b,) for s in out]
    return out


def bits_of(n):
    out, b = [], 1
    while b < n:
        out.append(b)
        b *= 2
    return out


def peers(ndp, nfs):
    return nfs - 1 + len(bits_of(ndp))


class Plan:
    def __init__(self, ndp, nfs, send, recv, local):
        self.ndp, self.nfs, self.send, self.recv, self.lsem = ndp, nfs, send, recv, local
        self.dp, self.z = lax.axis_index(DP), lax.axis_index(FS)
        self.sent, self.locals = [], 0

    def barrier(self):
        sem = pltpu.get_barrier_semaphore()
        to = [(self.dp, (self.z + k) % self.nfs) for k in range(1, self.nfs)]
        to += [(flip(self.dp, b), self.z) for b in bits_of(self.ndp)]
        for dev in to:
            pl.semaphore_signal(sem, inc=1, device_id=dev, device_id_type=pl.DeviceIdType.MESH)
        pl.semaphore_wait(sem, len(to))

    def copy(self, src, dst, dp, z):
        n = len(self.sent)
        c = pltpu.make_async_remote_copy(
            src_ref=src, dst_ref=dst, send_sem=self.send.at[n], recv_sem=self.recv.at[n], device_id=(dp, z),
            device_id_type=pl.DeviceIdType.MESH,
        )
        self.sent.append(c)
        return c

    def here(self, src, dst):
        self.locals += 1
        return pltpu.make_async_copy(src, dst, self.lsem.at[self.locals - 1])

    def finish(self):
        for c in self.sent:
            c.wait_send()


def start(cs):
    for c in cs:
        c.start()


def arrive(cs):
    for c in cs:
        c.wait_recv()


def spread(plan, halves, slot, own, first, extra):
    k = len(halves[0][1])
    chips, sibs = [], []
    fresh = [(part_, ()) for part_, _ in halves]
    for s in range(k + 1):
        sibs.append([])
        for part_, sub in fresh:
            e = flips(plan.dp, sub)
            src = slot(part_, e) if sub else own(part_)
            sibs[-1].append(plan.copy(src, slot(part_, e), flip(plan.dp, 1), plan.z))
        if s == k:
            break
        chips.append([])
        for part_, order in halves:
            for sub in subsets(order[:s]):
                e = flips(plan.dp, sub)
                src = slot(part_, e) if sub else own(part_)
                chips[-1].append(plan.copy(src, slot(part_, e), flip(plan.dp, order[s]), plan.z))
        fresh = [(p_, sub + (order[s],)) for p_, order in halves for sub in subsets(order[:s])]

    def opening():
        first()
        if k:
            start(chips[0])
        start(sibs[0])

    def middle(s):
        def step():
            arrive(chips[s - 1])
            if s < k:
                start(chips[s])
            start(sibs[s])

        return step

    def closing():
        for group in sibs:
            arrive(group)
        extra()

    return [opening] + [middle(s) for s in range(1, k + 1)] + [closing]


def two_orders(ndp):
    bs = [2 * b for b in bits_of(ndp // 2)]
    return bs, bs[::-1]


def gather_steps(plan, shard, g, ready):
    nfs, n = plan.nfs, g.shape[1] // plan.ndp
    mine = shard.at[pl.ds(plan.dp * n, n), :]
    here = g.at[plan.z, pl.ds(plan.dp * n, n), :]
    own = plan.here(mine, here)
    zs = [plan.copy(mine, here, plan.dp, (plan.z + k) % nfs) for k in range(1, nfs)]
    hz = nfs // 2
    up, down = two_orders(plan.ndp)
    halves = [(pl.ds(0, hz), up), (pl.ds(hz, nfs - hz), down)]

    def slot(part_, e):
        return g.at[part_, pl.ds(e * n, n), :]

    def begin():
        ready()
        start(zs)
        own.start()

    def landed():
        own.wait()
        arrive(zs)

    rest = spread(plan, halves, slot, lambda p_: slot(p_, plan.dp), landed, lambda: None)
    return [begin] + rest


def place(cw, full, at, rows_first):
    a = lax.broadcasted_iota(jnp.int32, (cw, full) if rows_first else (full, cw), 0)
    b = lax.broadcasted_iota(jnp.int32, (cw, full) if rows_first else (full, cw), 1)
    hit = b == a + at if rows_first else a == b + at
    return jnp.where(hit, 1.0, 0.0).astype(BF)


def bias_gather_steps(plan, bl, zb, bias):
    nfs = plan.nfs
    nh, r, cw = bl.shape
    full = cw * nfs
    own = plan.here(bl, zb.at[plan.z])
    mine = pl.ds(pl.multiple_of(plan.dp * r, r), r)
    zs = [plan.copy(bl, zb.at[plan.z], plan.dp, (plan.z + k) % nfs) for k in range(1, nfs)]
    up, down = two_orders(plan.ndp)
    hh = nh // 2
    halves = [(pl.ds(0, hh), up), (pl.ds(hh, nh - hh), down)]

    def begin():
        own.start()
        start(zs)

    def join():
        own.wait()
        arrive(zs)

        def some(i, carry):
            total = None
            for zz in range(nfs):
                v = zb[zz, pl.ds(i * 8, 8)].reshape(8 * r, cw)
                term = dot(v, place(cw, full, zz * cw, True))
                total = term if total is None else total + term
            bias[pl.ds(i * 8, 8), mine, :] = total.astype(BF).reshape(8, r, full)
            return carry

        lax.fori_loop(0, nh // 8, some, 0)

    def slot(p_, e):
        return bias.at[p_, pl.ds(e * r, r), :]

    rest = spread(plan, halves, slot, lambda p_: slot(p_, plan.dp), join, lambda: None)
    return [begin] + rest


def add_rows(dst, src):
    def one(i, carry):
        dst[i] = dst[i] + src[i]
        return carry

    lax.fori_loop(0, dst.shape[0], one, 0)


def sum_steps(plan, piece, acc, crecv, rbuf, cut, ready):
    nchip = acc.shape[0]
    dp, z = plan.dp, plan.z
    m, core = dp // 2, dp % 2
    cs = [plan.copy(piece(2 * f + 1 - core), crecv.at[f], flip(dp, 1), z) for f in range(nchip)]
    ls = [plan.here(piece(2 * f + core), acc.at[f]) for f in range(nchip)]
    bs = bits_of(nchip)
    orders = (bs, bs[::-1])
    rounds = []
    at = [0, 0]
    for s in range(len(bs)):
        rounds.append([])
        for h, order in enumerate(orders):
            part_ = pl.ds(*cut[h])
            for sub in subsets(order[s + 1 :]):
                f = flips(m, (order[s],) + sub)
                c = plan.copy(acc.at[f, part_], rbuf.at[at[h], part_], flip(dp, 2 * order[s]), z)
                rounds[-1].append((c, flips(m, sub), at[h], part_))
                at[h] += 1

    def begin():
        ready()
        start(cs)
        start(ls)

    def pair():
        for f in range(nchip):
            ls[f].wait()
            cs[f].wait_recv()
            add_rows(acc.at[f], crecv.at[f])
        if rounds:
            start([c[0] for c in rounds[0]])

    def chip(s):
        def step():
            for c, f, o, part_ in rounds[s - 1]:
                c.wait_recv()
                add_rows(acc.at[f, part_], rbuf.at[o, part_])
            if s < len(bs):
                start([c[0] for c in rounds[s]])

        return step

    return [begin, pair] + [chip(s) for s in range(1, len(bs) + 1)]


def join_steps(one, two):
    def both():
        one[-1]()
        two[0]()

    return one[:-1] + [both] + two[1:]


def reduce_steps(plan, pg, out, acc, crecv, rbuf, zr, fin, ready):
    nfs, n = plan.nfs, acc.shape[2]
    dp, z = plan.dp, plan.z
    hz = nfs // 2
    sums = sum_steps(plan, lambda e: pg.at[:, pl.ds(e * n, n), :], acc, crecv, rbuf, ((0, hz), (hz, nfs - hz)), ready)
    zs = [plan.copy(acc.at[dp // 2, (z + k) % nfs], zr.at[k - 1], dp, (z + k) % nfs) for k in range(1, nfs)]
    keep = plan.here(fin, out.at[pl.ds(dp * n, n), :])
    w = fin.shape[1] // 2
    up, down = two_orders(plan.ndp)
    halves = [(pl.ds(0, w), up), (pl.ds(w, w), down)]

    def total():
        arrive(zs)
        t = acc[dp // 2, z].astype(F32)
        for k in range(nfs - 1):
            t = t + zr[k].astype(F32)
        fin[...] = t.astype(BF)
        keep.start()

    rest = spread(plan, halves, lambda p_, e: out.at[pl.ds(e * n, n), p_], lambda p_: fin.at[:, p_], total, keep.wait)
    return join_steps(sums, [lambda: start(zs)]) + rest


def bias_reduce_steps(plan, db, out, acc, crecv, rbuf, zs, zr):
    nfs = plan.nfs
    dp, z = plan.dp, plan.z
    nchip, nh, r, full = acc.shape
    cw = full // nfs
    hh = nh // 2
    sums = sum_steps(plan, lambda e: db.at[:, pl.ds(e * r, r), :], acc, crecv, rbuf, ((0, hh), (hh, nh - hh)), lambda: None)
    to = [plan.copy(zs.at[(z + k) % nfs], zr.at[k - 1], dp, (z + k) % nfs) for k in range(1, nfs)]

    def cut():
        def some(i, carry):
            v = acc[dp // 2, pl.ds(i * 8, 8)].reshape(8 * r, full)
            for zz in range(nfs):
                zs[zz, pl.ds(i * 8, 8)] = dot(v, place(cw, full, zz * cw, False)).astype(BF).reshape(8, r, cw)
            return carry

        lax.fori_loop(0, nh // 8, some, 0)
        start(to)

    def total():
        arrive(to)

        def one(i, carry):
            t = zs[z, i].astype(F32)
            for k in range(nfs - 1):
                t = t + zr[k, i].astype(F32)
            out[i] = t.astype(BF).astype(F32)
            return carry

        lax.fori_loop(0, nh, one, 0)

    return join_steps(sums, [cut]) + [total]


DMA = pltpu.SemaphoreType.DMA


def pair_params(tg):
    m = tg[...].reshape(128, 128)
    rows = dot_tn(m, place(128, 128, 0, True))
    return rows[0:16].astype(BF), rows[16:17]


def pair_rows(pair, n, i):
    x = pair[n, pl.ds(i * 16, 16)].astype(F32)
    return norm(x.reshape(x.shape[0] * x.shape[1], x.shape[2]))


def pair_steps(plan, pair, tp, tg, bl):
    nfs = plan.nfs
    ncomp, r, cw, _ = pair.shape
    zs = [plan.copy(tp, tg.at[plan.z], plan.dp, (plan.z + k) % nfs) for k in range(1, nfs)]

    def begin():
        tg[plan.z] = tp[...]
        start(zs)

    def work(n):
        def step():
            if n == 0:
                arrive(zs)
            pw, gain = pair_params(tg)
            heads = pw.shape[0]

            def some(i, carry):
                pn, _ = pair_rows(pair, n, i)
                low = (pn * gain).astype(BF)
                parts = [dot_nt(pw, low[cw * k : cw * k + cw]) for k in range(16)]
                v = jnp.transpose(jnp.stack(parts), (1, 0, 2))
                bl[pl.ds(n * heads, heads), pl.ds(i * 16, 16), :] = v.astype(BF)
                return carry

            lax.fori_loop(0, r // 16, some, 0)

        return step

    return [begin] + [work(n) for n in range(ncomp)]


def pair_back(pair_hbm, tg, ob, pgrad, tacc):
    ncomp, r, cw, width = pair_hbm.shape
    pw, gain = pair_params(tg)
    heads = pw.shape[0]
    per = r // 16

    def run(pair, pgb, lsem, osem):
        load = pltpu.make_async_copy(pair_hbm, pair, lsem.at[0])
        load.start()
        load.wait()

        def flight(it):
            return pltpu.make_async_copy(pgb.at[it % 2], pgrad.at[it // per, pl.ds(it % per * 16, 16)], osem.at[it % 2])

        def some(it, carry):
            pwg, pgg = carry
            n, i = it // per, it % per
            pn, pr = pair_rows(pair, n, i)
            low = (pn * gain).astype(BF)
            g = jnp.transpose(ob[pl.ds(n * heads, heads), pl.ds(i * 16, 16), :], (1, 0, 2)).astype(BF)
            parts = []
            for k in range(16):
                parts.append(dot_tn(g[k], pw))
                pwg = pwg + dot(g[k], low[cw * k : cw * k + cw])
            gl = jnp.concatenate(parts, axis=0)
            pgg = pgg + jnp.sum(gl * pn, axis=0, keepdims=True)

            @pl.when(it >= 2)
            def _():
                flight(it - 2).wait()

            pgb[it % 2] = norm_back(pn, pr, gl * gain).reshape(16, cw, width)
            flight(it).start()
            return pwg, pgg

        zero = (jnp.zeros((heads, width), F32), jnp.zeros((1, width), F32))
        pwg, pgg = lax.fori_loop(0, ncomp * per, some, zero)
        for it in range(max(ncomp * per - 2, 0), ncomp * per):
            flight(it).wait()
        tacc[0, 0:16, :] = pwg
        tacc[0, 16:32, :] = jnp.broadcast_to(pgg, (16, width))

    pl.run_scoped(run, pltpu.VMEM(pair_hbm.shape, BF), pltpu.VMEM((2, 16, cw, width), F32), DMA((1,)), DMA((2,)))


def tiny_steps(plan, tacc, tr, tz, out, work):
    nfs = plan.nfs
    bs = bits_of(plan.ndp)
    cs = [plan.copy(tacc.at[i], tr.at[i], flip(plan.dp, b), plan.z) for i, b in enumerate(bs)]
    zs = [plan.copy(tacc.at[len(bs)], tz.at[k - 1], plan.dp, (plan.z + k) % nfs) for k in range(1, nfs)]

    def begin():
        work()
        cs[0].start()

    def step(i):
        def go():
            cs[i].wait_recv()
            tacc[i + 1] = tacc[i] + tr[i]
            start([cs[i + 1]] if i + 1 < len(bs) else zs)

        return go

    def total():
        arrive(zs)
        t = tacc[len(bs)]
        for k in range(nfs - 1):
            t = t + tz[k]
        out[...] = t

    return [begin] + [step(i) for i in range(len(bs))] + [total]


ANYWHERE = pl.BlockSpec(memory_space=pl.ANY)
def follow(order, lists):
    at = {k: 0 for k in lists}
    for ch in order:
        if ch in lists and at[ch] < len(lists[ch]):
            lists[ch][at[ch]]()
            at[ch] += 1
    for k, steps in lists.items():
        for step in steps[at[k] :]:
            step()


VMEM = pl.BlockSpec(memory_space=pltpu.VMEM)
SMEM = pl.BlockSpec(memory_space=pltpu.SMEM)


WITHIN = 0


def fill_vectors(small, s1, rows1):
    parts = [v[...].astype(F32) for v in small]
    v = jnp.concatenate(parts[:5] + [jnp.concatenate(parts[5:], axis=1)], axis=0)
    pad = jnp.zeros((16 - v.shape[0], v.shape[1]), F32)
    s1[rows1 : rows1 + 16, 0 : v.shape[1]] = jnp.concatenate([v, pad], axis=0).astype(BF)


def forward_parts(plan, rows1, comp, cnt, x, c, g1, sm, outs, bias, wv, vs, pst, psem, fsem, during, within):
    nfs = plan.nfs
    copies = comp.shape[0]
    t, d = x.shape
    dc = c.shape[1]
    rows = t // copies
    dz, cz = d // nfs, dc // nfs
    heads = outs[-1].shape[1]
    groups = 2
    per, dg, hs = heads // groups, d // groups, d // heads
    load = plan.here(g1, wv)
    leave = [pltpu.make_async_copy(v, o, fsem.at[i]) for i, (v, o) in enumerate(zip(vs, outs))]
    fi, q, k, v, gp, sp, cl, att, gated = vs
    p = outs[-1]

    def vectors():
        parts = [jnp.zeros((16, d), F32), jnp.zeros((16, dc), F32), jnp.zeros((16, dc), F32)]
        a = lax.broadcasted_iota(jnp.int32, (dz, dc), 0)
        b = lax.broadcasted_iota(jnp.int32, (dz, dc), 1)
        for z in range(nfs):
            piece = wv[z, rows1 : rows1 + 16, :][:, :dz]
            one = jnp.where((a < cz) & (b == a + z * cz), 1.0, 0.0).astype(BF)
            two = jnp.where((a >= cz) & (b == a - cz + z * cz), 1.0, 0.0).astype(BF)
            for i, e in enumerate((place(dz, d, z * dz, True), one, two)):
                parts[i] = parts[i] + dot(piece, e)
        sm[...] = parts[0][0:8]
        sm[5:6, 0:dc] = parts[1][5:6]
        sm[6:7, 0:dc] = parts[2][5:6]

    def first():
        load.start()
        load.wait()
        vectors()

        def one(i, carry):
            at = pl.ds(pl.multiple_of(i * rows, rows), rows)

            def view(ref):
                return ref.at[at, :]

            ws = [wv.at[:, pl.ds(j * dz, dz), :] for j in range(4)]
            ws += [wv.at[:, pl.ds(4 * dz + j * cz, cz), :] for j in range(2)]
            first_kernel(view(x), view(c), *ws, sm, *[view(o) for o in vs[:7]])
            for at_i, step in during.items():
                pl.when(i == at_i)(step)
            return carry

        lax.fori_loop(0, copies, one, 0)
        start(leave[:7])

    def flight(it):
        return pltpu.make_async_copy(pst.at[it % 2], p.at[it // groups, pl.ds(it % groups * per, per)], psem.at[it % 2])

    def attend():
        def one(it, carry):
            ci, g = it // groups, it % groups
            at = pl.ds(pl.multiple_of(ci * rows, rows), rows)
            cols = pl.ds(pl.multiple_of(g * dg, dg), dg)
            n = comp[ci]

            @pl.when(it >= 2)
            def _():
                flight(it - 2).wait()

            def keep(j, val):
                pst[it % 2, j] = val

            def view(ref):
                return ref.at[at, cols]

            attend_body(per, hs, cnt[n], view(q), view(k), view(v), lambda j: bias[n * heads + g * per + j], view(gp),
                        keep, view(att), view(gated))
            flight(it).start()
            pl.when(it == WITHIN)(within)
            return carry

        lax.fori_loop(0, copies * groups, one, 0)
        start(leave[7:])

    def leaving():
        for it in range(copies * groups - 2, copies * groups):
            flight(it).wait()
        for o in leave:
            o.wait()

    return first, attend, leaving


def gather_kernel(ndp, nfs, spots, rows1, with_bias, *refs):
    nw = len(spots)
    ws, small, rest = refs[:nw], refs[nw : nw + 7], refs[nw + 7 :]
    if with_bias:
        pair, tp, comp, cnt, x, c, g1, g2, tg, sm = rest[:10]
        outs, rest = rest[10:20], rest[20:]
        s1, s2, bl, zb, bias, wv, pst = rest[:7]
        vs = rest[7:16]
        send, recv, local, psem, fsem = rest[16:]
    else:
        g1, g2, s1, s2, send, recv, local = rest
    plan = Plan(ndp, nfs, send, recv, local)
    fill = {0: [], 1: []}
    for w, (which, col, width, at) in zip(ws, spots):
        src = w if width == w.shape[1] else w.at[:, pl.ds(col, width)]
        fill[which].append(plan.here(src, (s1, s2)[which].at[pl.ds(at, w.shape[0]), :]))
    start(fill[0])
    start(fill[1])
    fill_vectors(small, s1, rows1)
    plan.barrier()

    def wait(cs):
        def go():
            for c in cs:
                c.wait()

        return go

    size1 = g1.shape[1]
    half = size1 // 2
    nothing = wait([])
    if half % (16 * ndp) == 0:
        spans = [pl.ds(0, half), pl.ds(half, half)]
    else:
        spans = [pl.ds(0, size1)]
    a = [gather_steps(plan, s1.at[sp_], g1.at[:, sp_], nothing if i else wait(fill[0])) for i, sp_ in enumerate(spans)]
    c_ = gather_steps(plan, s2, g2, wait(fill[1]))
    if not with_bias:
        follow("", dict(enumerate(a + [c_])))
        plan.finish()
        return
    p = pair_steps(plan, pair, tp, tg, bl)
    ncomp = cnt.shape[0]
    heads = bl.shape[0] // ncomp
    b = []
    for n in range(ncomp):
        hs = pl.ds(n * heads, heads)
        b.append(bias_gather_steps(plan, bl.at[hs], zb.at[:, hs], bias.at[hs]))

    def both(*steps):
        def go():
            for step in steps:
                step()

        return go

    during = {0: both(b[-1][1], c_[0], b[0][2])} if ncomp > 1 else {}
    first, attend, leaving = forward_parts(
        plan, rows1, comp, cnt, x, c, g1, sm, outs, bias, wv, vs, pst, psem, fsem, during, c_[2]
    )
    run = [p[0], a[0][0], p[1], a[0][1]]
    for more in a[1:]:
        run += [more[0]]
    run += p[2:]
    for more in a[1:]:
        run += [more[1]]
    run += [b[0][0]]
    for i in range(2, len(a[0]) - 1):
        run += [more[i] for more in a]
    if ncomp > 1:
        run += [b[0][1], b[1][0]] + [b_ for more in b[1:-1] for b_ in more[1:]]
        run += [more[-1] for more in a] + [first, b[0][3], b[-1][2], c_[1], b[-1][3], b[0][4], b[-1][4]]
    else:
        run += [b[0][1], c_[0]] + [more[-1] for more in a] + [first, b[0][2], c_[1]] + b[0][3:]
    for step in run + [attend] + c_[3:] + [leaving]:
        step()
    plan.finish()


def run_gather(ndp, nfs, spots, ws, small, more, size1, size2, d, heads, rows1):
    sds = jax.ShapeDtypeStruct
    count = 80 * max(ndp // 4, 2)
    outs = [sds((nfs, size1, d), BF), sds((nfs, size2, d), BF)]
    specs = [ANYWHERE] * 2
    scratch = [pltpu.VMEM((size1, d), BF), pltpu.VMEM((size2, d), BF)]
    sems = [DMA((count,)), DMA((count,)), DMA((len(ws) + 8,))]
    ins = list(ws) + list(small)
    in_specs = [VMEM] * len(ins)
    if more is not None:
        pair, tp, comp, cnt, x, c = more
        ncomp, r, cw, _ = pair.shape
        nh, rows, full = ncomp * heads, r * ndp, cw * nfs
        t, dc = c.shape
        ins += more
        in_specs += [VMEM, VMEM, SMEM, SMEM, VMEM, VMEM]
        kept = [(t, d)] * 6 + [(t, dc)] + [(t, d)] * 2
        outs += [sds((nfs,) + tp.shape, BF), sds((8, d), F32)] + [sds(k, BF) for k in kept]
        outs += [sds((comp.shape[0], heads, rows, rows), BF)]
        specs += [VMEM, VMEM] + [ANYWHERE] * (len(kept) + 1)
        scratch += [pltpu.VMEM((nh, r, cw), BF), pltpu.VMEM((nfs, nh, r, cw), BF), pltpu.VMEM((nh, rows, full), BF),
                    pltpu.VMEM((nfs, size1, d), BF), pltpu.VMEM((2, heads // 2, rows, rows), BF)]
        scratch += [pltpu.VMEM(k, BF) for k in kept]
        sems += [DMA((2,)), DMA((len(kept),))]
    return pl.pallas_call(
        functools.partial(gather_kernel, ndp, nfs, spots, rows1, more is not None),
        in_specs=in_specs,
        out_specs=specs,
        out_shape=outs,
        scratch_shapes=scratch + sems,
        compiler_params=params(61, collective_id=0, has_side_effects=True),
        name="gather",
    )(*ins)


class Tiles:
    def __init__(self, bufs, sems):
        self.bufs, self.sems = bufs, sems
        self.held = [None] * bufs.shape[0]
        self.copies = [None] * bufs.shape[0]
        self.used = [-1] * bufs.shape[0]

    def fetch(self, key, ref, col, width, now):
        if key in self.held:
            i = self.held.index(key)
            self.used[i] = now
            return i
        i = self.used.index(min(self.used))
        self.held[i], self.used[i] = key, now
        src = ref if width == ref.shape[1] else ref.at[:, pl.ds(col, width)]
        self.copies[i] = pltpu.make_async_copy(src, self.bufs.at[i, :, pl.ds(0, width)], self.sems.at[i])
        self.copies[i].start()
        return i

    def wait(self, i):
        if self.copies[i] is not None:
            self.copies[i].wait()
            self.copies[i] = None


def attend_back_phase(comp, p, ops_hbm, outs_hbm, db, during):
    copies, heads, rows, _ = p.shape
    t, d = ops_hbm[0].shape
    ncomp = db.shape[0]
    groups = 2
    per, dg, hs = heads // groups, d // groups, d // heads
    width = min(256, dg)
    scale = hs ** (-0.5)

    def run(ops, res, pb, dbs, isem, psem, dsem, rsem):
        inds = [[jnp.full((1, rows), jnp.where(comp[c] == n, 1.0, 0.0), F32).astype(BF) for n in range(ncomp)] for c in range(copies)]
        for g in range(groups):
            cols = pl.ds(g * dg, dg)
            loads = [pltpu.make_async_copy(a.at[:, cols], ops.at[i], isem.at[i]) for i, a in enumerate(ops_hbm)]
            start(loads)

            def fetch(j, slot):
                return pltpu.make_async_copy(p.at[:, g * per + j], pb.at[slot], psem.at[slot])

            def flight(j):
                return pltpu.make_async_copy(dbs.at[j % 2], db.at[:, g * per + j], dsem.at[j % 2])

            fetch(0, 0).start()
            for c in loads:
                c.wait()
            res[...] = jnp.zeros_like(res)

            def one(j, carry):
                slot = j % 2
                fetch(j, slot).wait()

                @pl.when(j + 1 < per)
                def _():
                    fetch(j + 1, 1 - slot).start()

                @pl.when(j >= 2)
                def _():
                    flight(j - 2).wait()

                w = jnp.minimum(j * hs // 128 * 128, dg - width)
                m = lane_mask(j * hs - w, hs, width)
                win = pl.ds(pl.multiple_of(w, 128), width)
                acc = [None] * ncomp
                for c in range(copies):
                    rs = pl.ds(c * rows, rows)
                    dam = ops[3, rs, win] * m
                    delta = jnp.sum(dam.astype(F32) * ops[4, rs, win].astype(F32), axis=-1, keepdims=True)
                    pj = pb[slot, c]
                    ds = (pj.astype(F32) * (dot_nt(dam, ops[2, rs, win]) - delta)).astype(BF)
                    res[2, rs, win] += dot_tn(pj, dam).astype(BF)
                    res[0, rs, win] += (dot(ds, ops[1, rs, win] * m) * scale).astype(BF)
                    res[1, rs, win] += (dot_tn(ds, ops[0, rs, win] * m) * scale).astype(BF)
                    for n in range(ncomp):
                        term = ds * inds[c][n]
                        acc[n] = term if acc[n] is None else acc[n] + term
                for n in range(ncomp):
                    dbs[slot, n] = acc[n]
                flight(j).start()
                for jj in range(per):
                    if (g, jj) in during:
                        pl.when(j == jj)(during[(g, jj)])
                return carry

            lax.fori_loop(0, per, one, 0)
            back = [pltpu.make_async_copy(res.at[i], o.at[:, cols], rsem.at[i]) for i, o in enumerate(outs_hbm)]
            start(back)
            for c in back + [flight(per - 2), flight(per - 1)]:
                c.wait()

    pl.run_scoped(
        run, pltpu.VMEM((5, t, dg), BF), pltpu.VMEM((3, t, dg), BF), pltpu.VMEM((2, copies, rows, rows), BF),
        pltpu.VMEM((2, ncomp, rows, rows), BF), DMA((5,)), DMA((2,)), DMA((2,)), DMA((3,)),
    )


def last_phase(rows_hbm, c, gm, dcp, g1, sm, vec, outs_hbm, tb, during):
    t, d = rows_hbm[0].shape
    dc = c.shape[1]
    nfs = g1.shape[0]
    dz, cz = d // nfs, dc // nfs
    count = t // tb

    def run(wv, b6, cb, gmb, dcb, sgb, cgb, gsb, wsem, isem, osem):
        load = pltpu.make_async_copy(g1, wv, wsem.at[0])
        load.start()

        def come(i):
            at, k = pl.ds(pl.multiple_of(i * tb, tb), tb), i % 2
            pairs = [(r_.at[at, :], b6.at[k, n]) for n, r_ in enumerate(rows_hbm)]
            pairs += [(c.at[at, :], cb.at[k]), (gm.at[at, :], gmb.at[k]), (dcp.at[at, :], dcb.at[k])]
            return [pltpu.make_async_copy(a, b_, isem.at[k, n]) for n, (a, b_) in enumerate(pairs)]

        def leave(i):
            at, k = pl.ds(pl.multiple_of(i * tb, tb), tb), i % 2
            bufs = [sgb.at[k], cgb.at[k], gsb.at[k, 0], gsb.at[k, 1]]
            return [pltpu.make_async_copy(b_, o.at[at, :], osem.at[k, n]) for n, (b_, o) in enumerate(zip(bufs, outs_hbm))]

        start(come(0))
        vec[...] = jnp.zeros_like(vec)
        load.wait()
        ws = [wv.at[:, pl.ds(j * dz, dz), :] for j in range(4)]
        ws += [wv.at[:, pl.ds(4 * dz + j * cz, cz), :] for j in range(2)]

        def one(i, carry):
            k = i % 2
            for c_ in come(i):
                c_.wait()

            @pl.when(i + 1 < count)
            def _():
                start(come(i + 1))

            @pl.when(i >= 2)
            def _():
                for c_ in leave(i - 2):
                    c_.wait()

            r6 = [b6.at[k, n] for n in range(6)]
            last_body(*r6[:5], cb.at[k], r6[5], gmb.at[k], dcb.at[k], *ws, sm, sgb.at[k], cgb.at[k], gsb.at[k, 0],
                      gsb.at[k, 1], vec)
            start(leave(i))
            for ii in range(count):
                if ii in during:
                    pl.when(i == ii)(during[ii])
            return carry

        lax.fori_loop(0, count, one, 0)
        for i in range(max(count - 2, 0), count):
            for c_ in leave(i):
                c_.wait()

    pl.run_scoped(
        run, pltpu.VMEM(g1.shape, BF), pltpu.VMEM((2, 6, tb, d), BF), pltpu.VMEM((2, tb, dc), BF),
        pltpu.VMEM((2, tb, d), F32), pltpu.VMEM((2, tb, dc), F32), pltpu.VMEM((2, tb, d), F32), pltpu.VMEM((2, tb, dc), F32),
        pltpu.VMEM((2, 2, tb, d), BF), DMA((1,)), DMA((2, 9)), DMA((2, 4)),
    )


def cuts(size, unit):
    if size % (2 * unit) == 0:
        return [(0, size // 2), (size // 2, size // 2)]
    return [(0, size)]


ROWS = 384
LAST = 128
ORDERS = (
    "jjjjjSjjSjjjjT",
    {(0, 1): "T", (0, 5): "S", (1, 2): "S", (1, 6): "T"},
    {0: "b", 1: "c", 2: "T", 3: "S", 6: "b", 7: "T"},
    "ScjjjQbjQTjSjRc",
    "RSTQbRQcRtSTQRtttQRtSTQRSTQRSTQRSTQR",
)


def products_phase(jobs, ins, packs, order, step, state):
    t, d = ins[0].shape[0], packs[0].shape[2]
    nz = packs[0].shape[0]

    def run(tiles, outs, tsem, osem):
        held = Tiles(tiles, tsem)
        flying = [[] for _ in range(outs.shape[0])]
        ready = {}

        def operands(j):
            (li, lc, lw), (ri, rc, rw), _, _ = jobs[j]
            return (
                held.fetch((li, lc), ins[li], lc, lw, 2 * j),
                held.fetch((ri, rc), ins[ri], rc, rw, 2 * j + 1),
            )

        def job(j):
            if j not in ready:
                ready[j] = operands(j)
            (_, _, lw), _, which, (z0, count, (zr, at)) = jobs[j]
            li, ri = ready[j]
            held.wait(li)
            held.wait(ri)
            if j + 1 < len(jobs):
                ready[j + 1] = operands(j + 1)
            o = j % outs.shape[0]
            for c in flying[o]:
                c.wait()
            kb = min(lw, ROWS)

            def some(i, carry):
                cols = pl.ds(pl.multiple_of(i * kb, kb), kb)
                outs[o, cols, :] = dot_tn(tiles[li, :, cols], tiles[ri]).astype(BF)
                return carry

            lax.fori_loop(0, lw // kb, some, 0)
            flying[o] = [
                pltpu.make_async_copy(
                    outs.at[o, pl.ds(i * zr, zr), :], packs[which].at[z0 + i, pl.ds(at, zr), :], osem.at[o, i]
                )
                for i in range(count)
            ]
            start(flying[o])

        def settle():
            for o in range(outs.shape[0]):
                for c in flying[o]:
                    c.wait()
                flying[o] = []

        state["settle"] = settle
        j = 0
        for ch in order:
            if ch == "j":
                job(j)
                j += 1
            else:
                step(ch)
        settle()
        state["settle"] = lambda: None

    pl.run_scoped(run, pltpu.VMEM((4, t, d), BF), pltpu.VMEM((2, d, d), BF), DMA((4,)), DMA((2, nz)))


def products_kernel(ndp, nfs, jobs, split, orders, nin, small_at, cuts1, cuts2, full, *refs):
    ins, rest = list(refs[:nin]), list(refs[nin:])

    def take(n):
        out = rest[:n]
        del rest[:n]
        return out

    if full:
        p, q, k, v, da, att, x, c, sp, gm, dcp, g1, sm, vec_a, comp, pair, tg = take(17)
    else:
        (small,) = take(1)
    r1, r2, pg1, pg2 = take(4)
    if full:
        dq, dk, dv, gsc, gsh, db, sg, cg, pgrad, tiny_out = take(10)
    per = 5
    bufs1 = [take(per) for _ in cuts1]
    bufs2 = [take(per) for _ in cuts2]
    send, recv, local = take(3)
    if full:
        small, vec = take(2)
        ins += [dq, dk, dv, gsc, gsh]
    plan = Plan(ndp, nfs, send, recv, local)
    state = {"settle": lambda: None}
    lsmall = plan.here(small, pg1.at[:, pl.ds(small_at, 16), :])

    def settle():
        state["settle"]()

    def settle_small():
        settle()
        if full:
            both = jnp.concatenate([vec_a[...] + vec[...], jnp.zeros_like(vec)], axis=0).astype(BF)
            d, dc = x.shape[1], c.shape[1]
            dz, cz = d // nfs, dc // nfs
            row = lax.broadcasted_iota(jnp.int32, (16, 1), 0)
            small[...] = jnp.zeros_like(small)
            for z in range(nfs):
                wide = dot(both, place(dz, d, z * dz, False))
                thin = dot(both[:, :dc], place(dz, dc, z * cz, False))
                small[z, :, 0:dz] = jnp.where((row == 5) | (row == 6), thin, wide).astype(BF)
        lsmall.start()
        lsmall.wait()

    def chunks(pg, out, bufs, spans, last):
        done = []
        for i, (buf, span) in enumerate(zip(bufs, spans)):
            at = pl.ds(*span)
            done.append(reduce_steps(plan, pg.at[:, at], out.at[at], *buf, last if i == len(bufs) - 1 else settle))
        return done

    lists = {"STU"[i]: steps for i, steps in enumerate(chunks(pg2, r2, bufs2, cuts2, settle))}
    lists.update({"QR"[i]: steps for i, steps in enumerate(chunks(pg1, r1, bufs1, cuts1, settle_small))})
    if full:
        (ob,) = take(1)
        ncomp = db.shape[0]
        heads = ob.shape[0] // ncomp
        for n in range(ncomp):
            lists["bc"[n]] = bias_reduce_steps(plan, db.at[n], ob.at[pl.ds(n * heads, heads)], *take(5))
        tacc, tr, tz = take(3)
        lists["t"] = tiny_steps(plan, tacc, tr, tz, tiny_out, lambda: pair_back(pair, tg, ob, pgrad, tacc))
    left = {name: list(steps) for name, steps in lists.items()}

    def step(ch):
        if left.get(ch):
            left[ch].pop(0)()

    def steps_of(table):
        return {key: (lambda chs: lambda: [step(ch) for ch in chs] and None)(chs) for key, chs in table.items()}

    first, in_attend, in_last, second, tail = orders
    plan.barrier()
    products_phase(jobs[:split], ins, (pg1, pg2), first, step, state)
    if full:
        attend_back_phase(comp, p, (q, k, v, da, att), (dq, dk, dv), db, steps_of(in_attend))
        step("b")
        step("c")
        last_phase((dq, dk, dv, ins[14], x, sp), c, gm, dcp, g1, sm, vec, (sg, cg, gsc, gsh), LAST, steps_of(in_last))
    products_phase(jobs[split:], ins, (pg1, pg2), second, step, state)
    for ch in tail:
        step(ch)
    for name in left:
        while left[name]:
            step(name)
    plan.finish()


def run_products(ndp, nfs, jobs, split, orders, ins, more, small, small_at, size1, size2):
    t = ins[0].shape[0]
    d = ins[1].shape[1]
    nchip = ndp // 2
    sds = jax.ShapeDtypeStruct

    def sums(*shape):
        return [pltpu.VMEM((nchip,) + shape, BF), pltpu.VMEM((nchip,) + shape, BF), pltpu.VMEM((max(nchip - 1, 1),) + shape, BF)]

    cuts1, cuts2 = cuts(size1, 16 * ndp), cuts(size2, 16 * ndp)

    def scratch(spans):
        got = []
        for _, size in spans:
            n = size // ndp
            got += sums(nfs, n, d) + [pltpu.VMEM((nfs - 1, n, d), BF), pltpu.VMEM((n, d), BF)]
        return got

    count = 100 * max(ndp // 4, 2)
    outs = [sds((size1, d), BF), sds((size2, d), BF), sds((nfs, size1, d), BF), sds((nfs, size2, d), BF)]
    out_specs = [ANYWHERE] * 4
    in_specs = [ANYWHERE] * len(ins)
    tail_scratch = []
    if more is not None:
        p, pair, dc = more[0], more[15], more[7].shape[1]
        _, heads, rows, full = p.shape
        ncomp, r, cw, width = pair.shape
        levels = len(bits_of(ndp))
        in_specs += [ANYWHERE] * 12 + [VMEM, VMEM, SMEM, ANYWHERE, VMEM]
        extra = list(more)
        outs += [sds((t, d), BF)] * 5 + [sds((ncomp, heads, rows, full), BF), sds((t, d), F32), sds((t, dc), F32),
                                         sds(pair.shape, F32), sds((32, width), F32)]
        out_specs += [ANYWHERE] * 9 + [VMEM]
        tail_scratch = [pltpu.VMEM((nfs, 16, d), BF), pltpu.VMEM((8, d), F32), pltpu.VMEM((ncomp * heads, r, cw), F32)]
        tail_scratch += (sums(heads, r, full) + [pltpu.VMEM((nfs, heads, r, cw), BF), pltpu.VMEM((nfs - 1, heads, r, cw), BF)]) * ncomp
        tail_scratch += [pltpu.VMEM((k, 32, width), F32) for k in (levels + 1, levels, nfs - 1)]
    else:
        in_specs += [VMEM]
        extra = [small]
    return pl.pallas_call(
        functools.partial(products_kernel, ndp, nfs, jobs, split, orders, len(ins), small_at, cuts1, cuts2,
                          more is not None),
        in_specs=in_specs,
        out_specs=out_specs,
        out_shape=outs,
        scratch_shapes=scratch(cuts1) + scratch(cuts2)
        + [DMA((count,)), DMA((count,)), DMA((8 * nchip + 10,))] + tail_scratch,
        compiler_params=params(62, collective_id=1, has_side_effects=True),
        name="products",
    )(*ins, *extra)


def emit_kernel(spots, r1, r2, *outs):
    for o, (which, at) in zip(outs, spots):
        r = (r1, r2)[which]
        n = o.shape[0]
        for i, row in enumerate(at):
            w = r.shape[1]
            o[:, i * w : i * w + w] = r[row : row + n, :].astype(F32)


def run_emit(r1, r2, spots, shapes):
    sds = jax.ShapeDtypeStruct
    return pl.pallas_call(
        functools.partial(emit_kernel, spots),
        in_specs=[VMEM] * 2,
        out_specs=[VMEM] * len(shapes),
        out_shape=[sds(k, F32) for k in shapes],
        compiler_params=params(40),
        name="emit",
    )(r1, r2)


def body(ndp, nfs, *args):
    (single, condition, pair_tensor, counts, complex_of, cotangent, condition_gain, scale_weight, scale_bias,
     shift_weight, query_weight, query_bias, key_weight, value_weight, gate_weight, output_weight, pair_gain,
     pair_weight, branch_gate_weight, branch_gate_bias, transition_gain, transition_scale_weight,
     transition_scale_bias, transition_shift_weight, hidden_gate, hidden_value, hidden_output, final_gate_weight,
     final_gate_bias) = args
    copies, rows, d = single.shape
    dc = condition.shape[2]
    t = copies * rows
    heads = pair_weight.shape[1]
    ncomp = counts.shape[0]
    dz = d // nfs
    x = single.reshape(t, d)
    c = condition.reshape(t, dc)
    ct = cotangent.reshape(t, d)
    unit = 16 * ndp

    def padded(total):
        return -(-total // unit) * unit

    vectors = (scale_bias, query_bias, branch_gate_bias, transition_scale_bias, final_gate_bias,
               condition_gain, transition_gain)
    small = [v[None, :] for v in vectors]
    cz, fz = dc // nfs, hidden_output.shape[0]
    rows1 = 4 * dz + 2 * cz
    rows2 = fz + 5 * dz + 4 * cz
    size1, size2 = padded(rows1 + 16), padded(rows2)
    ws, spots = [], []

    def spot(w, which, at, col=0):
        ws.append(w)
        spots.append((which, col, d, at))

    for i, w in enumerate((query_weight, key_weight, value_weight, gate_weight)):
        spot(w, 0, i * dz)
    spot(scale_weight, 0, 4 * dz)
    spot(shift_weight, 0, 4 * dz + cz)
    spot(hidden_output, 1, 0)
    spot(output_weight, 1, fz)
    for i, (w, col) in enumerate(((hidden_gate, 0), (hidden_gate, d), (hidden_value, 0), (hidden_value, d))):
        spot(w, 1, fz + (i + 1) * dz, col)
    for i, w in enumerate((branch_gate_weight, transition_scale_weight, transition_shift_weight, final_gate_weight)):
        spot(w, 1, fz + 5 * dz + i * cz)
    pair_width = pair_weight.shape[0] * nfs
    local_rows, local_cols = pair_tensor.shape[1:3]
    pgw = jnp.concatenate([pair_weight, pair_gain[:, None]], axis=1)
    aligned = local_rows % 16 == 0 and heads == 16 and pair_width == 128
    if aligned:
        tp = jnp.pad(pgw, ((0, 0), (0, pair_width - heads - 1)))
        more = [pair_tensor, tp, complex_of, counts, x, c]
        g1, g2, tg, sm, first_in, q, k, v, gp, sp, cl1, att, gated, p = run_gather(
            ndp, nfs, tuple(spots), ws, small, more, size1, size2, d, heads, rows1
        )
    else:
        pgw = lax.all_gather(pgw, FS, axis=0, tiled=True)
        pw, pgain = pgw[:, :heads], pgw[:, heads].astype(F32)
        pair_norm, pair_rstd = norm(pair_tensor.astype(F32))
        pair_low = (pair_norm * pgain).astype(BF)
        bias_local = jnp.transpose(dot(pair_low, pw).astype(BF), (0, 3, 1, 2))
        g1, g2 = run_gather(ndp, nfs, tuple(spots), ws, small, None, size1, size2, d, heads, rows1)
        bias = lax.all_gather(bias_local, FS, axis=3, tiled=True)
        bias = lax.all_gather(bias, DP, axis=2, tiled=True)
        tg = None
        sm = jnp.transpose(g1[:, rows1 : rows1 + 8, :dz], (1, 0, 2)).reshape(8, d).astype(F32)
        gains = g1[:, rows1 + 5, : 2 * cz].reshape(nfs, 2, cz)
        gains = jnp.transpose(gains, (1, 0, 2)).reshape(2, dc).astype(F32)
        sm = jnp.concatenate([sm[:5], jnp.pad(gains, ((0, 0), (0, d - dc))), sm[7:]], axis=0)
        first_in, q, k, v, gp, sp, cl1 = run_first(x, c, g1, sm, rows)
        p, att, gated = run_attend(complex_of, counts, q, k, v, gp, bias, 2)

    (out, gm, dcp, si, act, cl2, gt2, gz2, gh, gv, gsc2, gsh2, gt1, gz1, da, dg, vec_a) = run_middle(
        complex_of, counts, x, c, ct, gated, att, gp, g2, sm, rows
    )
    small_grad = None
    if not aligned:
        dq, dk, dv, db = run_attend_back(complex_of, p, q, k, v, da, att, ncomp, 2)
        sgrad, cgrad, gsc1, gsh1, vec_b = run_last(dq, dk, dv, dg, x, c, sp, gm, dcp, g1, sm, rows)
        vec = (vec_a + vec_b).astype(BF)
        vz = jnp.transpose(vec.reshape(8, nfs, dz), (1, 0, 2))
        cv = jnp.transpose(vec[5:7, :dc].reshape(2, nfs, cz), (1, 0, 2))
        vz = jnp.concatenate(
            [vz[:, :5], jnp.pad(cv, ((0, 0), (0, 0), (0, dz - cz))), jnp.zeros((nfs, 9, dz), BF)], axis=1
        )
        small_grad = jnp.pad(vz, ((0, 0), (0, 0), (0, d - dz)))
    ins = [act, gt2, si, gh, gv, gated, gt1, c, gz1, gz2, cl2, gsc2, gsh2, first_in, dg, cl1]
    hz = nfs // 2

    def job(li, lc, lw, ri, rc, which, at):
        if lw == dc:
            where = (0, nfs, (cz, at))
        elif li == 0:
            where = (lc // d * hz, hz, (fz, at))
        else:
            where = (0, nfs, (dz, at))
        return ((li, lc, lw), (ri, rc, d), which, where)

    c0 = fz + 5 * dz
    jobs = [
        job(0, 0, d, 1, 0, 1, 0), job(0, d, d, 1, 0, 1, 0),
        job(2, 0, d, 3, 0, 1, fz + dz), job(2, 0, d, 3, d, 1, fz + 2 * dz),
        job(5, 0, d, 6, 0, 1, fz),
        job(2, 0, d, 4, 0, 1, fz + 3 * dz), job(2, 0, d, 4, d, 1, fz + 4 * dz),
        job(7, 0, dc, 8, 0, 1, c0), job(7, 0, dc, 9, 0, 1, c0 + 3 * cz),
        job(10, 0, dc, 11, 0, 1, c0 + cz), job(10, 0, dc, 12, 0, 1, c0 + 2 * cz),
        job(13, 0, d, 16, 0, 0, 0), job(13, 0, d, 17, 0, 0, dz), job(13, 0, d, 18, 0, 0, 2 * dz),
        job(13, 0, d, 14, 0, 0, 3 * dz),
        job(15, 0, dc, 19, 0, 0, 4 * dz), job(15, 0, dc, 20, 0, 0, 4 * dz + cz),
    ]
    if aligned:
        more = [p, q, k, v, da, att, x, c, sp, gm, dcp, g1, sm, vec_a, complex_of, pair_tensor, tg]
    else:
        more = None
        ins += [dq, dk, dv, gsc1, gsh1]
    moved = run_products(ndp, nfs, jobs, 11, ORDERS, ins, more, small_grad, rows1, size1, size2)
    r1, r2 = moved[:2]
    pz = pair_width // nfs
    if aligned:
        sgrad, cgrad, pair_grad = moved[10:13]
        tiny = lax.dynamic_slice_in_dim(moved[13][: heads + 1], lax.axis_index(FS) * pz, pz, axis=1).T
    else:
        bias_sum = lax.psum_scatter(db, DP, scatter_dimension=2, tiled=True)
        bias_sum = lax.psum_scatter(bias_sum, FS, scatter_dimension=3, tiled=True)
        bias_grad = jnp.transpose(bias_sum, (0, 2, 3, 1))
        pw_grad = dot_tn(pair_low.reshape(-1, pair_width), bias_grad.reshape(-1, heads))
        grad_low = dot(bias_grad, pw.T)
        pgain_grad = jnp.sum(grad_low * pair_norm, axis=(0, 1, 2))
        pair_grad = norm_back(pair_norm, pair_rstd, grad_low * pgain)
        tiny = lax.psum(jnp.concatenate([pw_grad, pgain_grad[:, None]], axis=1), (DP, FS))
        tiny = lax.dynamic_slice_in_dim(tiny, lax.axis_index(FS) * pz, pz, axis=0)
    sv = r1[rows1 : rows1 + 8].astype(F32)
    at = fz + 5 * dz
    spots = tuple((0, (i * dz,)) for i in range(4)) + tuple((0, (4 * dz + i * cz,)) for i in range(2))
    spots += ((1, (fz,)), (1, (fz + dz, fz + 2 * dz)), (1, (fz + 3 * dz, fz + 4 * dz)), (1, (0,)))
    spots += tuple((1, (at + i * cz,)) for i in range(4))
    shapes = [(dz, d)] * 4 + [(cz, d)] * 2 + [(dz, d), (dz, 2 * d), (dz, 2 * d), (fz, d)] + [(cz, d)] * 4
    w = run_emit(r1, r2, spots, shapes)
    o1, s1, o2, c2 = w[:4], w[4:6], w[6:10], w[10:]
    shape3 = (copies, rows, d)
    return (
        out.reshape(shape3),
        sgrad.reshape(shape3),
        cgrad.reshape(copies, rows, dc),
        pair_grad,
        sv[5, :cz],
        s1[0],
        sv[0, :dz],
        s1[1],
        o1[0],
        sv[1, :dz],
        o1[1],
        o1[2],
        o1[3],
        o2[0],
        tiny[:, heads],
        tiny[:, :heads],
        c2[0],
        sv[2, :dz],
        sv[6, :cz],
        c2[1],
        sv[3, :dz],
        c2[2],
        o2[1],
        o2[2],
        o2[3],
        c2[3],
        sv[4, :dz],
    )


def solution(mesh):
    both = (DP, FS)
    wide = P(both, None, None)
    mat = P(FS, None)
    vec = P(FS)
    pair = P(None, DP, FS, None)
    weights = (vec, mat, vec, mat, mat, vec, mat, mat, mat, mat, vec, mat, mat, vec, vec, mat, vec, mat, mat, mat,
               mat, mat, vec)
    in_specs = (wide, wide, pair, P(), P(both), wide) + weights
    out_specs = (wide, wide, wide, pair) + weights
    run = functools.partial(body, mesh.shape[DP], mesh.shape[FS])
    return jax.shard_map(run, mesh=mesh, in_specs=in_specs, out_specs=out_specs, check_vma=False)
```
